512 devices in a mesh: tm: 64 (over x, z), row: 4 (over y), col: 2 (over core).
Axes of the slice: x: 4, y: 4, z: 16, core: 2. Of those that a mesh axis runs over, the one named last changes fastest.
Arguments:
- inputs: bfloat16 [64, 64, 64, 128], P('tm', 'row', 'col'), may hold values from -6 to 6
- cotangent: bfloat16 [64, 64, 64, 128], P('tm', 'row', 'col'), may hold values from -6 to 6
- w_in: bfloat16 [3, 3, 128, 256], replicated, may hold values from -0.1875 to 0.1875
- w_out: bfloat16 [3, 3, 256, 128], replicated, may hold values from -0.125 to 0.125
- decay: float32 [64, 256], P('tm'), may hold values from 0.35 to 1
- skip: float32 [128], replicated, may hold values from -1 to 1
Outputs:
- d_inputs: bfloat16 [64, 64, 64, 128], P('tm', 'row', 'col')
- d_in_conv: float32 [256, 3, 3, 128], P('tm')
- d_out_conv: float32 [256, 3, 3, 128], P('tm')
- decay_gradient: float32 [64, 256], P('tm')
The draws below stay inside these ranges and needn't reach their ends.
All inputs are finite; a program needn't handle non-finite values.
Results may differ from the reference program's by a relative error of at most 0.017.
Values may be sent and summed in bfloat16 or wider, within the bound.
A program may use at most 192 MiB of HBM per device.

```python
import math
import jax
import jax.numpy as jnp
from jax import lax

H = 128
P_SIZE = 256
GH = 64
GW = 64
SPAN_SNAPSHOTS = 64


def draw_decay(key, part):
    key = jax.random.fold_in(key, 11)
    sampler_seeds = jax.random.split(key, 6)
    share = 0.5
    slow = jax.random.uniform(sampler_seeds[0], (P_SIZE,)) < share
    slow_rate = jnp.exp(jax.random.uniform(sampler_seeds[1], (P_SIZE,), jnp.float32, math.log(0.0002), math.log(0.003)))
    fast_rate = jnp.exp(jax.random.uniform(sampler_seeds[2], (P_SIZE,), jnp.float32, math.log(0.05), math.log(0.15)))
    rate = jnp.where(slow, slow_rate, fast_rate)
    step_len = jnp.exp(jax.random.uniform(sampler_seeds[3], (SPAN_SNAPSHOTS, 1), jnp.float32, math.log(0.5), math.log(2.0)))
    spike_clusters = jax.random.randint(sampler_seeds[4], (3,), 0, SPAN_SNAPSHOTS)
    flagged_snapshots = jnp.any(jnp.arange(SPAN_SNAPSHOTS)[:, None] == spike_clusters[None, :], axis=1, keepdims=True)
    keep = jax.random.uniform(sampler_seeds[5], (SPAN_SNAPSHOTS, P_SIZE), jnp.float32, 0.5, 0.8)
    return jnp.exp(-rate[None, :] * step_len) * jnp.where(flagged_snapshots, keep, 1.0)


def levels(key, extent, shards, least, high):
    def one(axis_at, parts):
        heights = jax.random.uniform(jax.random.fold_in(jax.random.fold_in(key, 6), axis_at), (parts,), jnp.float32, least / len(shards), high / len(shards))
        return jnp.repeat(jnp.exp(heights), extent[axis_at] // parts).reshape((-1,) + (1,) * (len(extent) - axis_at - 1))

    factor_of = one(*shards[0])
    for cut in shards[1:]:
        factor_of = factor_of * one(*cut)
    return factor_of


def centred(own_key, dims, width, most, pieces=(), held_as=jnp.bfloat16):
    loudness = levels(own_key, dims, pieces, -0.22, 0.18) if pieces else 1.0
    entries = jax.random.normal(own_key, dims, jnp.float32) * width * loudness
    return jnp.minimum(jnp.maximum(entries, -most), most).astype(held_as)


def setup_inputs(seed: int = 0) -> dict:
    key_of = jax.random.split(jax.random.key(seed), 7)
    return {
        "inputs": centred(key_of[0], (SPAN_SNAPSHOTS, GH, GW, H), 1.0, 6.0, ((0, 64), (1, 4), (2, 2))),
        "cotangent": centred(key_of[1], (SPAN_SNAPSHOTS, GH, GW, H), 1.0, 6.0, ((0, 64), (1, 4), (2, 2))),
        "w_in": centred(key_of[2], (3, 3, H, P_SIZE), (9 * H) ** -0.5, 0.1875),
        "w_out": centred(key_of[3], (3, 3, P_SIZE, H), (9 * P_SIZE) ** -0.5, 0.125),
        "decay": draw_decay(jax.random.fold_in(key_of[6], 71), 0),
        "skip": jnp.clip(jax.random.uniform(key_of[5], (H,), jnp.float32, -1.0, 1.0), -1.0, 1.0),
    }


def pad_grid(field):
    return jnp.pad(field, ((1, 1), (1, 1), (0, 0)))

def filtered_snapshot(padded, weight):
    rows = padded.shape[0] - 2
    cols = padded.shape[1] - 2
    total = jnp.zeros((rows * cols, weight.shape[3]), jnp.float32)
    for di in range(3):
        for dj in range(3):
            piece = padded[di:di + rows, dj:dj + cols].reshape(rows * cols, -1)
            total = total + jnp.dot(piece, weight[di, dj], preferred_element_type=jnp.float32)
    return total.reshape(rows, cols, -1)

def conv_frame_t(padded, weight):
    rows = padded.shape[0] - 2
    cols = padded.shape[1] - 2
    total = jnp.zeros((rows * cols, weight.shape[2]), jnp.float32)
    for di in range(3):
        for dj in range(3):
            piece = padded[2 - di:2 - di + rows, 2 - dj:2 - dj + cols].reshape(rows * cols, -1)
            total = total + jnp.dot(piece, weight[di, dj].T, preferred_element_type=jnp.float32)
    return total.reshape(rows, cols, -1)

def reference(inputs, cotangent, w_in, w_out, decay, skip):
    wscale = 1.0 / math.sqrt(SPAN_SNAPSHOTS * GH * GW)
    multiplier_adjoint = 1.0 / math.sqrt(GH * GW)
    decay_next = jnp.concatenate([decay[1:], jnp.zeros((1, P_SIZE), jnp.float32)], axis=0)

    def backward(adjoint, items):
        cot_frame, rate = items
        adjoint = conv_frame_t(pad_grid(cot_frame), w_out) + rate * adjoint
        return (adjoint, adjoint)
    _, adjoints = lax.scan(backward, jnp.zeros((GH, GW, P_SIZE), jnp.float32), (cotangent, decay_next), reverse=True)

    def forward_pass(carry, items):
        state_prev, acc_in, acc_out = carry
        in_frame, cot_frame, rate, adjoint = items
        in_pad = pad_grid(in_frame)
        cot_pad = pad_grid(cot_frame)
        state = rate * state_prev + filtered_snapshot(in_pad, w_in)
        state_b = state.astype(jnp.bfloat16)
        adjoint_b = adjoint.astype(jnp.bfloat16)
        grad_in = conv_frame_t(pad_grid(adjoint_b), w_in) + skip * cot_frame.astype(jnp.float32)
        grad_decay = multiplier_adjoint * lax.optimization_barrier(jnp.sum(adjoint * state_prev, axis=(0, 1)))
        flat_adj = adjoint_b.reshape(GH * GW, P_SIZE).T
        flat_state = state_b.reshape(GH * GW, P_SIZE).T
        terms_in = []
        outgoing_terms = []
        for di in range(3):
            for dj in range(3):
                inp = in_pad[di:di + GH, dj:dj + GW].reshape(GH * GW, H)
                terms_in.append(jnp.dot(flat_adj, inp, preferred_element_type=jnp.float32))
                cot = cot_pad[2 - di:2 - di + GH, 2 - dj:2 - dj + GW].reshape(GH * GW, H)
                outgoing_terms.append(jnp.dot(flat_state, cot, preferred_element_type=jnp.float32))
        acc_in = acc_in + jnp.stack(terms_in, axis=1).reshape(P_SIZE, 3, 3, H)
        acc_out = acc_out + jnp.stack(outgoing_terms, axis=1).reshape(P_SIZE, 3, 3, H)
        return ((state, acc_in, acc_out), (grad_in.astype(jnp.bfloat16), grad_decay))
    start = (jnp.zeros((GH, GW, P_SIZE), jnp.float32), jnp.zeros((P_SIZE, 3, 3, H), jnp.float32), jnp.zeros((P_SIZE, 3, 3, H), jnp.float32))
    (_, acc_in, acc_out), (d_inputs, decay_gradient) = lax.scan(forward_pass, start, (inputs, cotangent, decay, adjoints))
    return (d_inputs, acc_in * wscale, acc_out * wscale, decay_gradient)
```

```python
import functools
import math

import jax
import jax.numpy as jnp
from jax import lax
from jax.experimental import pallas as pl
from jax.experimental.pallas import tpu as pltpu
from jax.sharding import PartitionSpec as P

MESH = pl.DeviceIdType.MESH
F32 = jnp.float32
BF16 = jnp.bfloat16
X_CHIPS = 4
TAPS = [(di, dj) for di in range(3) for dj in range(3)]
SIDES = [(dr, dc) for dr in (-1, 0, 1) for dc in (-1, 0, 1) if dr or dc]


def dot(a, b, dims):
    return lax.dot_general(a, b, (dims, ((), ())), preferred_element_type=F32)


def exact_dot(a, b, dims):
    high = a.astype(BF16)
    rest = a - high.astype(F32)
    mid = rest.astype(BF16)
    low = (rest - mid.astype(F32)).astype(BF16)
    return dot(high, b, dims) + dot(mid, b, dims) + dot(low, b, dims)


def kernel(
    nx, nz, ny, rows, ln, wscale, dscale,
    in_ref, cot_ref, win_ref, wout_ref, dec_ref, skip_ref,
    dinp_ref, din_ref, dout_ref, dg_ref,
    t32, send_c, send_i, send_d, recv_c, recv_i, recv_d, dec_in, decp,
    pad_c, pad_i, pad_a, cols_c, cols_i, w_src, w_exc, w_back,
    exc, src,
    carry_a, carries_a, carry_s, carries_s, entry, dg_part,
    grad, grad_b, from_core, part_b, from_y, part_y, part_yb, from_x,
    mail, from_z, share, shares,
    p1_send, p1_recv, halo_send, halo_recv, car_send, car_recv,
    core_sem, y_send, y_recv, x_send, x_recv, ag_send, ag_recv,
):
    cells = 2 * rows
    wide = 2 * nz
    states = 2 * ln
    block = cells * nz
    tm = lax.axis_index("tm")
    y = lax.axis_index("row")
    c = lax.axis_index("col")
    x = tm // nz
    z = tm % nz
    q = 2 * z + c
    home = q // nz
    place = q % nz
    paired = home == c
    spot = 2 * y + c

    def here(dr, dc):
        return (y + dr >= 0) & (y + dr < ny) & (q + dc >= 0) & (q + dc < wide)

    def beside(dr, dc):
        to = q + dc
        return (x * nz + to // 2, y + dr, to % 2)

    def spot_id(o):
        to = (spot + o) % (2 * ny)
        return (tm, to // 2, to % 2)

    pad_c[...] = jnp.zeros_like(pad_c)
    pad_i[...] = jnp.zeros_like(pad_i)
    pad_a[...] = jnp.zeros_like(pad_a)

    barrier = pltpu.get_barrier_semaphore()

    def greet(device):
        pl.semaphore_signal(barrier, inc=1, device_id=device, device_id_type=MESH)

    @pl.loop(0, nz)
    def _(t):
        @pl.when(jnp.logical_not(paired & (t == z)))
        def _():
            greet((x * nz + t, y, home))

    beside_count = jnp.int32(0)
    for dr, dc in SIDES:
        beside_count += here(dr, dc).astype(jnp.int32)

        @pl.when(here(dr, dc))
        def _():
            greet(beside(dr, dc))

    for o in range(1, nx):
        greet((((x + o) % nx) * nz + z, y, c))
    for o in range(1, 2 * ny):
        greet(spot_id(o))

    def pack(ref, out):
        t32[...] = ref[...].astype(F32).reshape(block, ln)

        @pl.loop(0, nz)
        def _(k):
            for col in range(2):
                out[k, col * rows : (col + 1) * rows] = t32[
                    pl.ds(2 * k + col, rows, stride=wide)
                ].astype(BF16)

    def scatter(at, source, target):
        @pl.loop(0, nz)
        def _(o):
            k = (z + o) % nz
            to = c * nz + k

            @pl.when(to == q)
            def _():
                pltpu.make_async_copy(source(k), target.at[z], p1_recv.at[at]).start()

            @pl.when(to != q)
            def _():
                pltpu.make_async_remote_copy(
                    source(k), target.at[z], p1_send.at[at], p1_recv.at[at],
                    device_id=(x * nz + to // 2, y, to % 2), device_id_type=MESH,
                ).start()

    def give_back(at, source, target):
        @pl.loop(0, nz)
        def _(o):
            t = (z + o) % nz
            own = paired & (t == z)

            @pl.when(own)
            def _():
                pltpu.make_async_copy(source.at[t], target.at[place], p1_recv.at[at]).start()

            @pl.when(jnp.logical_not(own))
            def _():
                pltpu.make_async_remote_copy(
                    source.at[t], target.at[place], p1_send.at[at], p1_recv.at[at],
                    device_id=(x * nz + t, y, home), device_id_type=MESH,
                ).start()

    def arrived(at, target):
        pltpu.make_async_copy(target, target, p1_recv.at[at]).wait()

    def sent(at, like):
        @pl.when(paired)
        def _():
            part = like.at[pl.ds(0, nz - 1)]
            pltpu.make_async_copy(part, part, p1_send.at[at]).wait()

        @pl.when(jnp.logical_not(paired))
        def _():
            pltpu.make_async_copy(like, like, p1_send.at[at]).wait()

    pack(cot_ref, send_c)
    pl.semaphore_wait(
        barrier, nz - paired.astype(jnp.int32) + beside_count + (nx - 1) + (2 * ny - 1)
    )
    scatter(0, lambda k: dec_ref, dec_in)
    scatter(1, lambda k: send_c.at[k], recv_c)
    pack(in_ref, send_i)
    scatter(2, lambda k: send_i.at[k], recv_i)

    old = lax.broadcasted_iota(jnp.int32, (states, states), 0)
    new = lax.broadcasted_iota(jnp.int32, (states, states), 1)
    perm = jnp.where((old % ny) * (nx * nz) + old // ny == new, 1.0, 0.0).astype(BF16)

    @pl.loop(0, 9)
    def _(tap):
        at = pl.ds(pl.multiple_of(tap * ln, ln), ln)
        w_src[at] = dot(win_ref[tap], perm, ((1,), (0,))).astype(BF16)
        w_exc[at] = dot(wout_ref[tap], perm, ((0,), (0,))).astype(BF16)
        w_back[tap] = dot(perm, win_ref[tap], ((0,), (1,))).astype(BF16)

    arrived(0, dec_in)
    rates = exact_dot(dec_in[...].reshape(nz, states), perm, ((1,), (0,)))
    decp[0] = rates[:, :ln]
    decp[1] = rates[:, ln:]

    def unpack(recv, pad):
        t32[...] = recv[...].astype(F32).reshape(block, ln)

        @pl.loop(0, rows)
        def _(r):
            for col in range(2):
                pad[1 + col, 1 + r] = t32[
                    pl.ds(col * rows + r, nz, stride=cells)
                ].astype(BF16)

    def halo(which, pad, act):
        for at, (dr, dc) in enumerate(SIDES):
            there = (-dr, -dc)
            from_rows = {-1: pl.ds(1, 1), 0: pl.ds(1, rows), 1: pl.ds(rows, 1)}[dr]
            to_rows = {-1: pl.ds(rows + 1, 1), 0: pl.ds(1, rows), 1: pl.ds(0, 1)}[dr]
            from_cols = {-1: pl.ds(1, 1), 0: pl.ds(1, 2), 1: pl.ds(2, 1)}[dc]
            to_cols = {-1: pl.ds(3, 1), 0: pl.ds(1, 2), 1: pl.ds(0, 1)}[dc]
            copy = pltpu.make_async_remote_copy(
                pad.at[from_cols, from_rows], pad.at[to_cols, to_rows],
                halo_send.at[which, at], halo_recv.at[which, at],
                device_id=beside(dr, dc), device_id_type=MESH,
            )
            if act == "send":
                pl.when(here(dr, dc))(copy.start)
            elif act == "sent":
                pl.when(here(dr, dc))(copy.wait_send)
            else:
                pl.when(here(*there))(copy.wait_recv)

    def lay_out(pad, cols, flip):
        for tap, (di, dj) in enumerate(TAPS):
            a, b = (2 - di, 2 - dj) if flip else (di, dj)
            cols[:, tap * ln : (tap + 1) * ln] = pad[b : b + 2, a : a + rows].reshape(block, ln)

    def carry_copy(send, recv, which, to):
        return pltpu.make_async_remote_copy(
            send, recv.at[x], car_send.at[which, to], car_recv.at[which, x],
            device_id=(to * nz + z, y, c), device_id_type=MESH,
        )

    def carry_from(recv, which, source):
        return pltpu.make_async_copy(recv.at[source], recv.at[source], car_recv.at[which, source])

    def fold(recv, which, order, needed):
        entry[...] = jnp.zeros_like(entry)
        for source in order:
            @pl.when(needed(source))
            def _():
                carry_from(recv, which, source).wait()
                for h in range(2):
                    entry[h] = (
                        recv[source, h, :cells] + recv[source, h, cells : cells + 1] * entry[h]
                    )

    frame = lambda t: pl.ds(t, cells, stride=nz)

    arrived(1, recv_c)
    unpack(recv_c, pad_c)
    halo(0, pad_c, "send")
    halo(0, pad_c, "arrive")
    lay_out(pad_c, cols_c, True)
    value = dot(cols_c[...], w_exc[...], ((1,), (0,)))
    exc[0] = value[:, :ln]
    exc[1] = value[:, ln:]

    for h in range(2):
        def adjoint_step(i, held):
            b, factor = held
            t = nz - 1 - i
            rate = decp[h, pl.ds(t, 1)]
            return rate * (exc[h, frame(t)] + b), factor * rate

        b, factor = lax.fori_loop(
            0, nz, adjoint_step, (jnp.zeros((cells, ln), F32), jnp.ones((1, ln), F32))
        )
        carry_a[h, :cells] = b
        carry_a[h, cells:] = jnp.broadcast_to(factor, (8, ln))
    for to in range(nx):
        pl.when(to < x)(carry_copy(carry_a, carries_a, 0, to).start)

    arrived(2, recv_i)
    unpack(recv_i, pad_i)
    halo(1, pad_i, "send")

    fold(carries_a, 0, range(nx - 1, -1, -1), lambda source: source > x)
    for h in range(2):
        def adjoint_final(i, b):
            t = nz - 1 - i
            level = exc[h, frame(t)] + b
            exc[h, frame(t)] = level
            return decp[h, pl.ds(t, 1)] * level

        lax.fori_loop(0, nz, adjoint_final, entry[h])
    adjoint_b = jnp.concatenate([exc[0], exc[1]], axis=1).astype(BF16)
    pad_a[1:3, 1 : 1 + rows] = adjoint_b.reshape(2, rows, nz, states)
    halo(2, pad_a, "send")

    halo(1, pad_i, "arrive")
    lay_out(pad_i, cols_i, False)
    value = dot(cols_i[...], w_src[...], ((1,), (0,)))
    src[0] = value[:, :ln]
    src[1] = value[:, ln:]
    for h in range(2):
        def state_step(t, level):
            return decp[h, pl.ds(t, 1)] * level + src[h, frame(t)]

        carry_s[h, :cells] = lax.fori_loop(0, nz, state_step, jnp.zeros((cells, ln), F32))
        carry_s[h, cells:] = carry_a[h, cells:]
    for to in range(nx):
        pl.when(to > x)(carry_copy(carry_s, carries_s, 1, to).start)

    def core_copy():
        return pltpu.make_async_remote_copy(
            grad_b, from_core, core_sem.at[0], core_sem.at[1],
            device_id=(tm, y, 1 - c), device_id_type=MESH,
        )

    grad[0] = dot(
        pad_a[1:3, 1 : 1 + rows].reshape(block, states), cols_i[...], ((0,), (0,))
    ).reshape(grad.shape[1:])

    @pl.when(c == 1)
    def _():
        grad_b[...] = grad[0].astype(BF16)
        core_copy().start()

    halo(2, pad_a, "arrive")
    total = skip_ref[...] * pad_c[1:3, 1 : 1 + rows].reshape(block, ln).astype(F32)
    for tap, (di, dj) in enumerate(TAPS):
        a, b = 2 - di, 2 - dj
        total += dot(pad_a[b : b + 2, a : a + rows].reshape(block, states), w_back[tap], ((1,), (0,)))
    t32[...] = total

    @pl.loop(0, nz)
    def _(t):
        send_d[t] = t32[frame(t)].astype(BF16)

    give_back(3, send_d, recv_d)

    fold(carries_s, 1, range(nx), lambda source: source < x)
    for h in range(2):
        def state_final(t, level):
            now = decp[h, pl.ds(t, 1)] * level + src[h, frame(t)]
            src[h, frame(t)] = now
            dg_part[h, pl.ds(t, 1)] = jnp.sum(exc[h, frame(t)] * level, axis=0, keepdims=True)
            return now

        lax.fori_loop(0, nz, state_final, entry[h])
    state_b = jnp.concatenate([src[0], src[1]], axis=1).astype(BF16)
    grad[1] = dot(state_b, cols_c[...], ((0,), (0,))).reshape(grad.shape[1:])

    @pl.when(c == 0)
    def _():
        grad_b[...] = grad[1].astype(BF16)
        core_copy().start()

    core_copy().wait_recv()

    def y_copy(o):
        to = (y + o) % ny
        return pltpu.make_async_remote_copy(
            part_b.at[to], from_y.at[o - 1], y_send.at[o - 1], y_recv.at[o - 1],
            device_id=(tm, to, c), device_id_type=MESH,
        )

    part_b[...] = (grad[c] + from_core[...].astype(F32)).astype(BF16)
    for o in range(1, ny):
        y_copy(o).start()

    arrived(3, recv_d)
    t32[...] = recv_d[...].astype(F32).reshape(block, ln)

    @pl.loop(0, rows)
    def _(r):
        dinp_ref[r] = t32[pl.ds(r, wide, stride=rows)].astype(BF16)

    dg_old = exact_dot(
        jnp.concatenate([dg_part[0], dg_part[1]], axis=1), perm, ((1,), (1,))
    )
    mail[:, 9] = dg_old[:, :ln]
    mail[:, 10] = dg_old[:, ln:]

    summed = grad[c, y] + from_core[y].astype(F32)
    for o in range(1, ny):
        y_copy(o).wait_recv()
        summed += from_y[o - 1].astype(F32)
    part_y[...] = summed.reshape(part_y.shape)
    part_yb[...] = summed.astype(BF16).reshape(part_y.shape)

    def x_copy(o):
        to = (x + o) % nx
        return pltpu.make_async_remote_copy(
            part_yb.at[to], from_x.at[o - 1], x_send.at[o - 1], x_recv.at[o - 1],
            device_id=(to * nz + z, y, c), device_id_type=MESH,
        )

    for o in range(1, nx):
        x_copy(o).start()
    summed = part_y[x]
    for o in range(1, nx):
        x_copy(o).wait_recv()
        summed += from_x[o - 1].astype(F32)
    for tap in range(9):
        mail[:, tap] = summed[:, tap * ln : (tap + 1) * ln]

    give_back(4, mail, from_z)
    arrived(4, from_z)
    both = [jnp.zeros((11, ln), F32), jnp.zeros((11, ln), F32)]
    for k in range(nz):
        both[k % 2] = both[k % 2] + from_z[k]
    share[:9] = both[0][:9]
    share[9:18] = both[1][:9]
    share[18:20] = both[0][9:] + both[1][9:]

    def share_copy(o):
        return pltpu.make_async_remote_copy(
            share, shares.at[spot], ag_send.at[o - 1], ag_recv.at[o - 1],
            device_id=spot_id(o), device_id_type=MESH,
        )

    for o in range(1, 2 * ny):
        share_copy(o).start()
    shares[spot] = share[...]
    for o in range(1, 2 * ny):
        share_copy(o).wait_recv()
    for j in range(ny):
        din_ref[j] = (shares[2 * j, :9] + shares[2 * j + 1, :9]) * wscale
        dout_ref[j] = (shares[2 * j, 9:18] + shares[2 * j + 1, 9:18]) * wscale
    total = shares[0, 18:20]
    for s in range(1, 2 * ny):
        total += shares[s, 18:20]
    dg_ref[...] = total * dscale

    sent(0, dec_in)
    sent(1, send_c)
    sent(2, send_i)
    sent(3, send_d)
    sent(4, mail)
    for which, pad in enumerate((pad_c, pad_i, pad_a)):
        halo(which, pad, "sent")
    for to in range(nx):
        pl.when(to < x)(carry_copy(carry_a, carries_a, 0, to).wait_send)
        pl.when(to > x)(carry_copy(carry_s, carries_s, 1, to).wait_send)
    core_copy().wait_send()
    for o in range(1, ny):
        y_copy(o).wait_send()
    for o in range(1, nx):
        x_copy(o).wait_send()
    for o in range(1, 2 * ny):
        share_copy(o).wait_send()


def body(nx, inputs, cotangent, w_in, w_out, decay, skip):
    _, rows, wide, ln = inputs.shape
    ny = lax.axis_size("row")
    nz = lax.axis_size("tm") // nx
    states = w_in.shape[3]
    cells = 2 * rows
    block = cells * nz
    wscale = 1.0 / math.sqrt(nx * nz * ny * rows * wide * 2)
    dscale = 1.0 / math.sqrt(ny * rows * wide * 2)
    vmem = pltpu.VMEM
    dma = pltpu.SemaphoreType.DMA
    scratch = [
        vmem((block, ln), F32),
        vmem((nz, cells, ln), BF16),
        vmem((nz, cells, ln), BF16),
        vmem((nz, cells, ln), BF16),
        vmem((nz, cells, ln), BF16),
        vmem((nz, cells, ln), BF16),
        vmem((nz, cells, ln), BF16),
        vmem((nz, 1, states), F32),
        vmem((2, nz, ln), F32),
        vmem((4, rows + 2, nz, ln), BF16),
        vmem((4, rows + 2, nz, ln), BF16),
        vmem((4, rows + 2, nz, states), BF16),
        vmem((block, 9 * ln), BF16),
        vmem((block, 9 * ln), BF16),
        vmem((9 * ln, states), BF16),
        vmem((9 * ln, states), BF16),
        vmem((9, states, ln), BF16),
        vmem((2, block, ln), F32),
        vmem((2, block, ln), F32),
        vmem((2, cells + 8, ln), F32),
        vmem((nx, 2, cells + 8, ln), F32),
        vmem((2, cells + 8, ln), F32),
        vmem((nx, 2, cells + 8, ln), F32),
        vmem((2, cells, ln), F32),
        vmem((2, nz, ln), F32),
        vmem((2, ny, nx * nz, 9 * ln), F32),
        vmem((ny, nx * nz, 9 * ln), BF16),
        vmem((ny, nx * nz, 9 * ln), BF16),
        vmem((ny, nx * nz, 9 * ln), BF16),
        vmem((ny - 1, nx * nz, 9 * ln), BF16),
        vmem((nx, nz, 9 * ln), F32),
        vmem((nx, nz, 9 * ln), BF16),
        vmem((nx - 1, nz, 9 * ln), BF16),
        vmem((nz, 11, ln), F32),
        vmem((nz, 11, ln), F32),
        vmem((20, ln), F32),
        vmem((2 * ny, 20, ln), F32),
        dma((5,)),
        dma((5,)),
        dma((3, 8)),
        dma((3, 8)),
        dma((2, nx)),
        dma((2, nx)),
        dma((2,)),
        dma((ny - 1,)),
        dma((ny - 1,)),
        dma((nx - 1,)),
        dma((nx - 1,)),
        dma((2 * ny - 1,)),
        dma((2 * ny - 1,)),
    ]
    d_inputs, d_in, d_out, d_decay = pl.pallas_call(
        functools.partial(kernel, nx, nz, ny, rows, ln, wscale, dscale),
        out_shape=(
            jax.ShapeDtypeStruct((rows, wide, ln), BF16),
            jax.ShapeDtypeStruct((ny, 9, ln), F32),
            jax.ShapeDtypeStruct((ny, 9, ln), F32),
            jax.ShapeDtypeStruct((2, ln), F32),
        ),
        in_specs=[pl.BlockSpec(memory_space=pltpu.VMEM)] * 6,
        out_specs=tuple([pl.BlockSpec(memory_space=pltpu.VMEM)] * 4),
        scratch_shapes=scratch,
        compiler_params=pltpu.CompilerParams(
            collective_id=0, has_side_effects=True, vmem_limit_bytes=48 * 1024 * 1024
        ),
        cost_estimate=pl.CostEstimate(
            flops=5 * 2 * block * 9 * ln * states, bytes_accessed=4 * 1024 * 1024, transcendentals=0
        ),
    )(
        inputs.reshape(rows, wide, ln),
        cotangent.reshape(rows, wide, ln),
        w_in.reshape(9, ln, states),
        w_out.reshape(9, states, ln),
        decay,
        skip.reshape(1, ln),
    )
    return (
        d_inputs[None],
        d_in.reshape(ny, 3, 3, ln),
        d_out.reshape(ny, 3, 3, ln),
        d_decay.reshape(1, states),
    )


def solution(mesh, nx=X_CHIPS):
    in_specs = (
        P("tm", "row", "col", None),
        P("tm", "row", "col", None),
        P(),
        P(),
        P("tm", None),
        P(),
    )
    out_specs = (
        P("tm", "row", "col", None),
        P("tm", None, None, None),
        P("tm", None, None, None),
        P("tm", None),
    )
    return jax.shard_map(
        functools.partial(body, nx), mesh=mesh, in_specs=in_specs, out_specs=out_specs,
        check_vma=False,
    )
```

```python
import functools
import math

import jax
import jax.numpy as jnp
from jax import lax
from jax.experimental import pallas as pl
from jax.experimental.pallas import tpu as pltpu
from jax.sharding import PartitionSpec as P

MESH = pl.DeviceIdType.MESH
F32 = jnp.float32
BF16 = jnp.bfloat16
X_CHIPS = 4
TAPS = [(di, dj) for di in range(3) for dj in range(3)]
SIDES = [(dr, dc) for dr in (-1, 0, 1) for dc in (-1, 0, 1) if dr or dc]


def dot(a, b, dims):
    return lax.dot_general(a, b, (dims, ((), ())), preferred_element_type=F32)


def exact_dot(a, b, dims):
    high = a.astype(BF16)
    rest = a - high.astype(F32)
    mid = rest.astype(BF16)
    low = (rest - mid.astype(F32)).astype(BF16)
    return dot(high, b, dims) + dot(mid, b, dims) + dot(low, b, dims)


def kernel(
    nx, nz, ny, rows, ln,
    in_hbm, cot_hbm, win_hbm, wout_hbm, dec_hbm, skip_hbm,
    dinp_hbm, shares,
    in_ref, cot_ref, win_ref, wout_ref, dec_ref, skip_ref, fetch_sem,
    t32, send_c, send_i, send_d, recv_c, recv_i, recv_d, dec_in, decp,
    pad_c, pad_i, pad_a, cols_c, cols_i, w_src, w_exc, w_back,
    exc, src,
    carry_a, carries_a, carry_s, carries_s, entry, dg_part,
    grad, grad_b, from_core, part_b, from_xy,
    mail32, mail, from_z, share, dinp_ref, put_sem,
    p1_send, p1_recv, halo_send, halo_recv, car_send, car_recv,
    core_sem, xy_send, xy_recv, ag_send, ag_recv,
):
    cells = 2 * rows
    wide = 2 * nz
    states = 2 * ln
    block = cells * nz
    tm = lax.axis_index("tm")
    y = lax.axis_index("row")
    c = lax.axis_index("col")
    x = tm // nz
    z = tm % nz
    q = 2 * z + c
    home = q // nz
    place = q % nz
    paired = home == c
    spot = 2 * y + c
    flat = x * ny + y

    def here(dr, dc):
        return (y + dr >= 0) & (y + dr < ny) & (q + dc >= 0) & (q + dc < wide)

    def beside(dr, dc):
        to = q + dc
        return (x * nz + to // 2, y + dr, to % 2)

    def flat_id(o):
        to = (flat + o) % (nx * ny)
        return ((to // ny) * nz + z, to % ny, c)

    def spot_id(o):
        to = (spot + o) % (2 * ny)
        return (tm, to // 2, to % 2)

    fetches = [
        pltpu.make_async_copy(source, target, fetch_sem.at[at])
        for at, (source, target) in enumerate([
            (cot_hbm, cot_ref), (in_hbm, in_ref), (dec_hbm, dec_ref),
            (wout_hbm, wout_ref), (win_hbm, win_ref), (skip_hbm, skip_ref),
        ])
    ]
    for fetch in fetches:
        fetch.start()

    barrier = pltpu.get_barrier_semaphore()

    def greet(device):
        pl.semaphore_signal(barrier, inc=1, device_id=device, device_id_type=MESH)

    @pl.loop(0, nz)
    def _(t):
        @pl.when(jnp.logical_not(paired & (t == z)))
        def _():
            greet((x * nz + t, y, home))

    @pl.loop(1, nx * ny)
    def _(o):
        greet(flat_id(o))

    for o in range(1, 2 * ny, 2):
        greet((tm, (y + o // 2) % ny, 1 - c))

    pad_c[...] = jnp.zeros_like(pad_c)
    pad_i[...] = jnp.zeros_like(pad_i)
    pad_a[...] = jnp.zeros_like(pad_a)

    beside_count = jnp.int32(0)
    for dr, dc in SIDES:
        beside_count += here(dr, dc).astype(jnp.int32)

        @pl.when(here(dr, dc))
        def _():
            greet(beside(dr, dc))


    def pack(ref, out):
        t32[...] = ref[...].astype(F32).reshape(block, ln)

        @pl.loop(0, nz)
        def _(k):
            for col in range(2):
                out[k, col * rows : (col + 1) * rows] = t32[
                    pl.ds(2 * k + col, rows, stride=wide)
                ].astype(BF16)

    def scatter(at, source, target):
        @pl.loop(0, nz)
        def _(o):
            k = (z + o) % nz
            to = c * nz + k

            @pl.when(to == q)
            def _():
                pltpu.make_async_copy(source(k), target.at[z], p1_recv.at[at]).start()

            @pl.when(to != q)
            def _():
                pltpu.make_async_remote_copy(
                    source(k), target.at[z], p1_send.at[at], p1_recv.at[at],
                    device_id=(x * nz + to // 2, y, to % 2), device_id_type=MESH,
                ).start()

    def give_back(at, source, target):
        @pl.loop(0, nz)
        def _(o):
            t = (z + o) % nz
            own = paired & (t == z)

            @pl.when(own)
            def _():
                pltpu.make_async_copy(source.at[t], target.at[place], p1_recv.at[at]).start()

            @pl.when(jnp.logical_not(own))
            def _():
                pltpu.make_async_remote_copy(
                    source.at[t], target.at[place], p1_send.at[at], p1_recv.at[at],
                    device_id=(x * nz + t, y, home), device_id_type=MESH,
                ).start()

    def arrived(at, target):
        pltpu.make_async_copy(target, target, p1_recv.at[at]).wait()

    def sent(at, like):
        @pl.when(paired)
        def _():
            part = like.at[pl.ds(0, nz - 1)]
            pltpu.make_async_copy(part, part, p1_send.at[at]).wait()

        @pl.when(jnp.logical_not(paired))
        def _():
            pltpu.make_async_copy(like, like, p1_send.at[at]).wait()

    fetches[0].wait()
    pack(cot_ref, send_c)
    pl.semaphore_wait(
        barrier, nz - paired.astype(jnp.int32) + beside_count + (nx * ny - 1) + ny
    )
    scatter(1, lambda k: send_c.at[k], recv_c)
    fetches[1].wait()
    pack(in_ref, send_i)
    fetches[2].wait()
    scatter(0, lambda k: dec_ref, dec_in)
    scatter(2, lambda k: send_i.at[k], recv_i)
    fetches[3].wait()
    fetches[4].wait()
    fetches[5].wait()

    old = lax.broadcasted_iota(jnp.int32, (states, states), 0)
    new = lax.broadcasted_iota(jnp.int32, (states, states), 1)
    perm = jnp.where((old % ny) * (nx * nz) + old // ny == new, 1.0, 0.0).astype(BF16)

    @pl.loop(0, 9)
    def _(tap):
        at = pl.ds(pl.multiple_of(tap * ln, ln), ln)
        w_src[at] = dot(win_ref[tap], perm, ((1,), (0,))).astype(BF16)
        w_exc[at] = dot(wout_ref[tap], perm, ((0,), (0,))).astype(BF16)
        w_back[tap] = dot(perm, win_ref[tap], ((0,), (1,))).astype(BF16)

    arrived(0, dec_in)
    rates = exact_dot(dec_in[...].reshape(nz, states), perm, ((1,), (0,)))
    decp[0] = rates[:, :ln]
    decp[1] = rates[:, ln:]

    def unpack(recv, pad):
        t32[...] = recv[...].astype(F32).reshape(block, ln)

        @pl.loop(0, rows)
        def _(r):
            for col in range(2):
                pad[1 + col, 1 + r] = t32[
                    pl.ds(col * rows + r, nz, stride=cells)
                ].astype(BF16)

    def halo(which, pad, act):
        for at, (dr, dc) in enumerate(SIDES):
            there = (-dr, -dc)
            from_rows = {-1: pl.ds(1, 1), 0: pl.ds(1, rows), 1: pl.ds(rows, 1)}[dr]
            to_rows = {-1: pl.ds(rows + 1, 1), 0: pl.ds(1, rows), 1: pl.ds(0, 1)}[dr]
            from_cols = {-1: pl.ds(1, 1), 0: pl.ds(1, 2), 1: pl.ds(2, 1)}[dc]
            to_cols = {-1: pl.ds(3, 1), 0: pl.ds(1, 2), 1: pl.ds(0, 1)}[dc]
            copy = pltpu.make_async_remote_copy(
                pad.at[from_cols, from_rows], pad.at[to_cols, to_rows],
                halo_send.at[which, at], halo_recv.at[which, at],
                device_id=beside(dr, dc), device_id_type=MESH,
            )
            if act == "send":
                pl.when(here(dr, dc))(copy.start)
            elif act == "sent":
                pl.when(here(dr, dc))(copy.wait_send)
            else:
                pl.when(here(*there))(copy.wait_recv)

    def lay_out(pad, cols, flip):
        for tap, (di, dj) in enumerate(TAPS):
            a, b = (2 - di, 2 - dj) if flip else (di, dj)
            cols[:, tap * ln : (tap + 1) * ln] = pad[b : b + 2, a : a + rows].reshape(block, ln)

    def carry_copy(send, recv, which, to):
        return pltpu.make_async_remote_copy(
            send, recv.at[x], car_send.at[which, to], car_recv.at[which, x],
            device_id=(to * nz + z, y, c), device_id_type=MESH,
        )

    def carry_from(recv, which, source):
        return pltpu.make_async_copy(recv.at[source], recv.at[source], car_recv.at[which, source])

    def fold(recv, which, order, needed):
        entry[...] = jnp.zeros_like(entry)
        for source in order:
            @pl.when(needed(source))
            def _():
                carry_from(recv, which, source).wait()
                for h in range(2):
                    entry[h] = (
                        recv[source, h, :cells] + recv[source, h, cells : cells + 1] * entry[h]
                    )

    frame = lambda t: pl.ds(t, cells, stride=nz)

    arrived(1, recv_c)
    unpack(recv_c, pad_c)
    halo(0, pad_c, "send")
    halo(0, pad_c, "arrive")
    lay_out(pad_c, cols_c, True)
    value = dot(cols_c[...], w_exc[...], ((1,), (0,)))
    exc[0] = value[:, :ln]
    exc[1] = value[:, ln:]

    for h in range(2):
        def adjoint_step(i, held):
            b, factor = held
            t = nz - 1 - i
            rate = decp[h, pl.ds(t, 1)]
            return rate * (exc[h, frame(t)] + b), factor * rate

        b, factor = lax.fori_loop(
            0, nz, adjoint_step, (jnp.zeros((cells, ln), F32), jnp.ones((1, ln), F32))
        )
        carry_a[h, :cells] = b
        carry_a[h, cells:] = jnp.broadcast_to(factor, (8, ln))
    for to in range(nx):
        pl.when(to < x)(carry_copy(carry_a, carries_a, 0, to).start)

    arrived(2, recv_i)
    unpack(recv_i, pad_i)
    halo(1, pad_i, "send")

    fold(carries_a, 0, range(nx - 1, -1, -1), lambda source: source > x)
    for h in range(2):
        def adjoint_final(i, b):
            t = nz - 1 - i
            level = exc[h, frame(t)] + b
            exc[h, frame(t)] = level
            return decp[h, pl.ds(t, 1)] * level

        lax.fori_loop(0, nz, adjoint_final, entry[h])
    adjoint_b = jnp.concatenate([exc[0], exc[1]], axis=1).astype(BF16)
    pad_a[1:3, 1 : 1 + rows] = adjoint_b.reshape(2, rows, nz, states)
    halo(2, pad_a, "send")

    halo(1, pad_i, "arrive")
    lay_out(pad_i, cols_i, False)
    value = dot(cols_i[...], w_src[...], ((1,), (0,)))
    src[0] = value[:, :ln]
    src[1] = value[:, ln:]
    for h in range(2):
        def state_step(t, level):
            return decp[h, pl.ds(t, 1)] * level + src[h, frame(t)]

        carry_s[h, :cells] = lax.fori_loop(0, nz, state_step, jnp.zeros((cells, ln), F32))
        carry_s[h, cells:] = carry_a[h, cells:]
    for to in range(nx):
        pl.when(to > x)(carry_copy(carry_s, carries_s, 1, to).start)

    def core_copy():
        return pltpu.make_async_remote_copy(
            grad_b, from_core, core_sem.at[0], core_sem.at[1],
            device_id=(tm, y, 1 - c), device_id_type=MESH,
        )

    grad[0] = dot(
        pad_a[1:3, 1 : 1 + rows].reshape(block, states), cols_i[...], ((0,), (0,))
    ).reshape(grad.shape[1:])

    def xy_copy(o):
        to = (flat + o) % (nx * ny)
        return pltpu.make_async_remote_copy(
            part_b.at[to % ny, to // ny], from_xy.at[o - 1], xy_send.at[o - 1], xy_recv.at[o - 1],
            device_id=flat_id(o), device_id_type=MESH,
        )

    def begin():
        core_copy().wait_recv()
        part_b[...] = (grad[c] + from_core[...].astype(F32)).astype(BF16)

        @pl.loop(1, nx * ny)
        def _(o):
            xy_copy(o).start()

    @pl.when(c == 1)
    def _():
        grad_b[...] = grad[0].astype(BF16)
        core_copy().start()

    pl.when(c == 0)(begin)

    fold(carries_s, 1, range(nx), lambda source: source < x)
    for h in range(2):
        def state_final(t, level):
            now = decp[h, pl.ds(t, 1)] * level + src[h, frame(t)]
            src[h, frame(t)] = now
            dg_part[h, pl.ds(t, 1)] = jnp.sum(exc[h, frame(t)] * level, axis=0, keepdims=True)
            return now

        lax.fori_loop(0, nz, state_final, entry[h])
    state_b = jnp.concatenate([src[0], src[1]], axis=1).astype(BF16)
    grad[1] = dot(state_b, cols_c[...], ((0,), (0,))).reshape(grad.shape[1:])

    @pl.when(c == 0)
    def _():
        grad_b[...] = grad[1].astype(BF16)
        core_copy().start()

    pl.when(c == 1)(begin)

    halo(2, pad_a, "arrive")
    total = skip_ref[...] * pad_c[1:3, 1 : 1 + rows].reshape(block, ln).astype(F32)
    for tap, (di, dj) in enumerate(TAPS):
        a, b = 2 - di, 2 - dj
        total += dot(pad_a[b : b + 2, a : a + rows].reshape(block, states), w_back[tap], ((1,), (0,)))
    t32[...] = total

    @pl.loop(0, nz)
    def _(t):
        send_d[t] = t32[frame(t)].astype(BF16)

    give_back(3, send_d, recv_d)

    arrived(3, recv_d)
    t32[...] = recv_d[...].astype(F32).reshape(block, ln)

    @pl.loop(0, rows)
    def _(r):
        dinp_ref[r] = t32[pl.ds(r, wide, stride=rows)].astype(BF16)

    put_dinp = pltpu.make_async_copy(dinp_ref, dinp_hbm, put_sem.at[0])
    put_dinp.start()

    dg_old = exact_dot(
        jnp.concatenate([dg_part[0], dg_part[1]], axis=1), perm, ((1,), (1,))
    )
    high = dg_old.astype(BF16).astype(F32)
    mid = (dg_old - high).astype(BF16).astype(F32)
    low = dg_old - high - mid
    mail32[:, 15] = jnp.zeros((nz, ln), F32)
    for at, part in enumerate((high, mid, low)):
        mail32[:, 9 + 2 * at] = part[:, :ln]
        mail32[:, 10 + 2 * at] = part[:, ln:]

    def xy_sum(o, total):
        xy_copy(o).wait_recv()
        return total + from_xy[o - 1].astype(F32)

    summed = lax.fori_loop(1, nx * ny, xy_sum, grad[c, y, x] + from_core[y, x].astype(F32))
    for tap in range(9):
        mail32[:, tap] = summed[:, tap * ln : (tap + 1) * ln]
    mail[...] = mail32[...].astype(BF16)

    give_back(4, mail, from_z)
    arrived(4, from_z)
    both = [jnp.zeros((16, ln), F32), jnp.zeros((16, ln), F32)]
    for k in range(nz):
        both[k % 2] = both[k % 2] + from_z[k].astype(F32)
    share[:9] = both[0][:9]
    share[9:18] = both[1][:9]
    rest = both[0] + both[1]
    share[18:20] = rest[9:11] + (rest[11:13] + rest[13:15])

    def share_copy(o):
        return pltpu.make_async_remote_copy(
            share, shares.at[spot], ag_send.at[o - 1], ag_recv.at[o - 1],
            device_id=spot_id(o), device_id_type=MESH,
        )

    for o in range(1, 2 * ny):
        share_copy(o).start()
    own = pltpu.make_async_copy(share, shares.at[spot], put_sem.at[1])
    own.start()
    for o in range(1, 2 * ny):
        share_copy(o).wait_recv()
    own.wait()
    put_dinp.wait()

    sent(0, dec_in)
    sent(1, send_c)
    sent(2, send_i)
    sent(3, send_d)
    sent(4, mail)
    for which, pad in enumerate((pad_c, pad_i, pad_a)):
        halo(which, pad, "sent")
    for to in range(nx):
        pl.when(to < x)(carry_copy(carry_a, carries_a, 0, to).wait_send)
        pl.when(to > x)(carry_copy(carry_s, carries_s, 1, to).wait_send)
    core_copy().wait_send()

    @pl.loop(1, nx * ny)
    def _(o):
        xy_copy(o).wait_send()

    for o in range(1, 2 * ny):
        share_copy(o).wait_send()


def finish(ny, ln, wscale, dscale, dinp_hbm, shares_hbm, out_hbm, din_ref, dout_ref, dg_ref, shares, tile, sem):
    fetch = pltpu.make_async_copy(shares_hbm, shares, sem.at[0])
    come = pltpu.make_async_copy(dinp_hbm, tile, sem.at[1])
    go = pltpu.make_async_copy(tile, out_hbm, sem.at[2])
    come.start()
    fetch.start()
    come.wait()
    go.start()
    fetch.wait()
    for j in range(ny):
        both = shares[2 * j] + shares[2 * j + 1]
        din_ref[:, j] = both[:9] * wscale
        dout_ref[:, j] = both[9:18] * wscale
    total = shares[0, 18:20]
    for s in range(1, 2 * ny):
        total += shares[s, 18:20]
    dg_ref[:, :ln] = total[:1] * dscale
    dg_ref[:, ln:] = total[1:] * dscale
    go.wait()


def body(nx, inputs, cotangent, w_in, w_out, decay, skip):
    _, rows, wide, ln = inputs.shape
    ny = lax.axis_size("row")
    nz = lax.axis_size("tm") // nx
    states = w_in.shape[3]
    cells = 2 * rows
    block = cells * nz
    wscale = 1.0 / math.sqrt(nx * nz * ny * rows * wide * 2)
    dscale = 1.0 / math.sqrt(ny * rows * wide * 2)
    vmem = pltpu.VMEM
    dma = pltpu.SemaphoreType.DMA
    scratch = [
        vmem((rows, wide, ln), BF16),
        vmem((rows, wide, ln), BF16),
        vmem((9, ln, states), BF16),
        vmem((9, states, ln), BF16),
        vmem((1, states), F32),
        vmem((1, ln), F32),
        dma((6,)),
        vmem((block, ln), F32),
        vmem((nz, cells, ln), BF16),
        vmem((nz, cells, ln), BF16),
        vmem((nz, cells, ln), BF16),
        vmem((nz, cells, ln), BF16),
        vmem((nz, cells, ln), BF16),
        vmem((nz, cells, ln), BF16),
        vmem((nz, 1, states), F32),
        vmem((2, nz, ln), F32),
        vmem((4, rows + 2, nz, ln), BF16),
        vmem((4, rows + 2, nz, ln), BF16),
        vmem((4, rows + 2, nz, states), BF16),
        vmem((block, 9 * ln), BF16),
        vmem((block, 9 * ln), BF16),
        vmem((9 * ln, states), BF16),
        vmem((9 * ln, states), BF16),
        vmem((9, states, ln), BF16),
        vmem((2, block, ln), F32),
        vmem((2, block, ln), F32),
        vmem((2, cells + 8, ln), F32),
        vmem((nx, 2, cells + 8, ln), F32),
        vmem((2, cells + 8, ln), F32),
        vmem((nx, 2, cells + 8, ln), F32),
        vmem((2, cells, ln), F32),
        vmem((2, nz, ln), F32),
        vmem((2, ny, nx, nz, 9 * ln), F32),
        vmem((ny, nx, nz, 9 * ln), BF16),
        vmem((ny, nx, nz, 9 * ln), BF16),
        vmem((ny, nx, nz, 9 * ln), BF16),
        vmem((nx * ny - 1, nz, 9 * ln), BF16),
        vmem((nz, 16, ln), F32),
        vmem((nz, 16, ln), BF16),
        vmem((nz, 16, ln), BF16),
        vmem((20, ln), F32),
        vmem((rows, wide, ln), BF16),
        dma((2,)),
        dma((5,)),
        dma((5,)),
        dma((3, 8)),
        dma((3, 8)),
        dma((2, nx)),
        dma((2, nx)),
        dma((2,)),
        dma((nx * ny - 1,)),
        dma((nx * ny - 1,)),
        dma((2 * ny - 1,)),
        dma((2 * ny - 1,)),
    ]
    tile = jax.ShapeDtypeStruct((rows, wide, ln), BF16)
    d_inputs, shares = pl.pallas_call(
        functools.partial(kernel, nx, nz, ny, rows, ln),
        out_shape=(tile, jax.ShapeDtypeStruct((2 * ny, 20, ln), F32)),
        in_specs=[pl.BlockSpec(memory_space=pltpu.HBM)] * 6,
        out_specs=(pl.BlockSpec(memory_space=pltpu.HBM), pl.BlockSpec(memory_space=pltpu.HBM)),
        scratch_shapes=scratch,
        compiler_params=pltpu.CompilerParams(
            collective_id=0, has_side_effects=True, vmem_limit_bytes=63 * 1024 * 1024
        ),
        cost_estimate=pl.CostEstimate(
            flops=5 * 2 * block * 9 * ln * states, bytes_accessed=4 * 1024 * 1024, transcendentals=0
        ),
    )(
        inputs.reshape(rows, wide, ln),
        cotangent.reshape(rows, wide, ln),
        w_in.reshape(9, ln, states),
        w_out.reshape(9, states, ln),
        decay,
        skip.reshape(1, ln),
    )
    whole = pl.BlockSpec(memory_space=pltpu.VMEM)
    d_inputs, d_in, d_out, d_decay = pl.pallas_call(
        functools.partial(finish, ny, ln, wscale, dscale),
        out_shape=(
            tile,
            jax.ShapeDtypeStruct((9, ny, ln), F32),
            jax.ShapeDtypeStruct((9, ny, ln), F32),
            jax.ShapeDtypeStruct((1, states), F32),
        ),
        in_specs=[pl.BlockSpec(memory_space=pltpu.HBM)] * 2,
        out_specs=(pl.BlockSpec(memory_space=pltpu.HBM), whole, whole, whole),
        scratch_shapes=[vmem((2 * ny, 20, ln), F32), vmem((rows, wide, ln), BF16), dma((3,))],
        compiler_params=pltpu.CompilerParams(vmem_limit_bytes=63 * 1024 * 1024),
    )(d_inputs, shares)

    def by_channel(grad):
        return jnp.transpose(grad.reshape(3, 3, ny, ln), (2, 0, 1, 3))

    return (d_inputs[None], by_channel(d_in), by_channel(d_out), d_decay)


def solution(mesh, nx=X_CHIPS):
    in_specs = (
        P("tm", "row", "col", None),
        P("tm", "row", "col", None),
        P(),
        P(),
        P("tm", None),
        P(),
    )
    out_specs = (
        P("tm", "row", "col", None),
        P("tm", None, None, None),
        P("tm", None, None, None),
        P("tm", None),
    )
    return jax.shard_map(
        functools.partial(body, nx), mesh=mesh, in_specs=in_specs, out_specs=out_specs,
        check_vma=False,
    )
```

```python
import functools
import math

import jax
import jax.numpy as jnp
from jax import lax
from jax.experimental import pallas as pl
from jax.experimental.pallas import tpu as pltpu
from jax.sharding import PartitionSpec as P

MESH = pl.DeviceIdType.MESH
F32 = jnp.float32
BF16 = jnp.bfloat16
X_CHIPS = 4
TAPS = [(di, dj) for di in range(3) for dj in range(3)]
SIDES = [(dr, dc) for dr in (-1, 0, 1) for dc in (-1, 0, 1) if dr or dc]


def dot(a, b, dims):
    return lax.dot_general(a, b, (dims, ((), ())), preferred_element_type=F32)


def exact_dot(a, b, dims):
    high = a.astype(BF16)
    rest = a - high.astype(F32)
    mid = rest.astype(BF16)
    low = (rest - mid.astype(F32)).astype(BF16)
    return dot(high, b, dims) + dot(mid, b, dims) + dot(low, b, dims)


def kernel(
    nx, nz, ny, rows, ln,
    in_hbm, cot_hbm, win_hbm, wout_hbm, dec_hbm, skip_hbm,
    dinp_hbm, shares,
    in_ref, cot_ref, win_ref, wout_ref, dec_ref, skip_ref, fetch_sem,
    t32, send_c, send_i, send_d, recv_c, recv_i, recv_d, dec_in, decp,
    pad_c, pad_i, pad_a, cols_c, cols_i, w_src, w_exc, w_back,
    exc, src,
    carry_a, carries_a, carry_s, carries_s, entry, dg_part,
    grad, grad_b, from_core, part_b, from_xy,
    mail32, mail, from_z, share, dinp_ref, put_sem,
    p1_send, p1_recv, halo_send, halo_recv, car_send, car_recv,
    core_sem, xy_send, xy_recv, ag_send, ag_recv,
):
    cells = 2 * rows
    wide = 2 * nz
    states = 2 * ln
    block = cells * nz
    tm = lax.axis_index("tm")
    y = lax.axis_index("row")
    c = lax.axis_index("col")
    x = tm // nz
    z = tm % nz
    q = 2 * z + c
    home = q // nz
    place = q % nz
    paired = home == c
    spot = 2 * y + c
    flat = x * ny + y

    def here(dr, dc):
        return (y + dr >= 0) & (y + dr < ny) & (q + dc >= 0) & (q + dc < wide)

    def beside(dr, dc):
        to = q + dc
        return (x * nz + to // 2, y + dr, to % 2)

    def flat_id(o):
        to = (flat + o) % (nx * ny)
        return ((to // ny) * nz + z, to % ny, c)

    def spot_id(o):
        to = (spot + o) % (2 * ny)
        return (tm, to // 2, to % 2)

    fetches = [
        pltpu.make_async_copy(source, target, fetch_sem.at[at])
        for at, (source, target) in enumerate([
            (cot_hbm, cot_ref), (in_hbm, in_ref), (dec_hbm, dec_ref),
            (wout_hbm, wout_ref), (win_hbm, win_ref), (skip_hbm, skip_ref),
        ])
    ]
    for fetch in fetches:
        fetch.start()

    barrier = pltpu.get_barrier_semaphore()

    def greet(device):
        pl.semaphore_signal(barrier, inc=1, device_id=device, device_id_type=MESH)

    @pl.loop(0, nz)
    def _(t):
        @pl.when(jnp.logical_not(paired & (t == z)))
        def _():
            greet((x * nz + t, y, home))

    @pl.loop(1, nx * ny)
    def _(o):
        greet(flat_id(o))

    for o in range(1, 2 * ny, 2):
        greet((tm, (y + o // 2) % ny, 1 - c))

    pad_c[...] = jnp.zeros_like(pad_c)
    pad_i[...] = jnp.zeros_like(pad_i)
    pad_a[...] = jnp.zeros_like(pad_a)

    beside_count = jnp.int32(0)
    for dr, dc in SIDES:
        beside_count += here(dr, dc).astype(jnp.int32)

        @pl.when(here(dr, dc))
        def _():
            greet(beside(dr, dc))


    def pack(ref, out):
        t32[...] = ref[...].astype(F32).reshape(block, ln)

        @pl.loop(0, nz)
        def _(k):
            for col in range(2):
                out[k, col * rows : (col + 1) * rows] = t32[
                    pl.ds(2 * k + col, rows, stride=wide)
                ].astype(BF16)

    def chip(i):
        odd = i % 2
        return (z + nz // 2 + (1 - odd) * (i // 2) - odd * ((i + 1) // 2) + nz) % nz

    def scatter(at, source, target):
        @pl.loop(0, nz)
        def _(i):
            to = chip(i)
            for core in range(2):
                k = 2 * to + core - c * nz
                wanted = (k >= 0) & (k < nz)
                own = (to == z) & (c == core)

                @pl.when(wanted & own)
                def _():
                    pltpu.make_async_copy(source(k), target.at[z], p1_recv.at[at]).start()

                @pl.when(wanted & jnp.logical_not(own))
                def _():
                    pltpu.make_async_remote_copy(
                        source(k), target.at[z], p1_send.at[at], p1_recv.at[at],
                        device_id=(x * nz + to, y, core), device_id_type=MESH,
                    ).start()

    def give_back(at, source, target):
        @pl.loop(0, nz)
        def _(i):
            t = chip(i)
            own = paired & (t == z)

            @pl.when(own)
            def _():
                pltpu.make_async_copy(source.at[t], target.at[place], p1_recv.at[at]).start()

            @pl.when(jnp.logical_not(own))
            def _():
                pltpu.make_async_remote_copy(
                    source.at[t], target.at[place], p1_send.at[at], p1_recv.at[at],
                    device_id=(x * nz + t, y, home), device_id_type=MESH,
                ).start()

    def arrived(at, target):
        pltpu.make_async_copy(target, target, p1_recv.at[at]).wait()

    def sent(at, like):
        @pl.when(paired)
        def _():
            part = like.at[pl.ds(0, nz - 1)]
            pltpu.make_async_copy(part, part, p1_send.at[at]).wait()

        @pl.when(jnp.logical_not(paired))
        def _():
            pltpu.make_async_copy(like, like, p1_send.at[at]).wait()

    fetches[0].wait()
    pack(cot_ref, send_c)
    pl.semaphore_wait(
        barrier, nz - paired.astype(jnp.int32) + beside_count + (nx * ny - 1) + ny
    )
    scatter(1, lambda k: send_c.at[k], recv_c)
    fetches[1].wait()
    pack(in_ref, send_i)
    fetches[2].wait()
    scatter(0, lambda k: dec_ref, dec_in)
    scatter(2, lambda k: send_i.at[k], recv_i)
    fetches[3].wait()
    fetches[4].wait()
    fetches[5].wait()

    old = lax.broadcasted_iota(jnp.int32, (states, states), 0)
    new = lax.broadcasted_iota(jnp.int32, (states, states), 1)
    perm = jnp.where((old % ny) * (nx * nz) + old // ny == new, 1.0, 0.0).astype(BF16)

    @pl.loop(0, 9)
    def _(tap):
        at = pl.ds(pl.multiple_of(tap * ln, ln), ln)
        w_src[at] = dot(win_ref[tap], perm, ((1,), (0,))).astype(BF16)
        w_exc[at] = dot(wout_ref[tap], perm, ((0,), (0,))).astype(BF16)
        w_back[tap] = dot(perm, win_ref[tap], ((0,), (1,))).astype(BF16)

    arrived(0, dec_in)
    rates = exact_dot(dec_in[...].reshape(nz, states), perm, ((1,), (0,)))
    decp[0] = rates[:, :ln]
    decp[1] = rates[:, ln:]

    def unpack(recv, pad):
        t32[...] = recv[...].astype(F32).reshape(block, ln)

        @pl.loop(0, rows)
        def _(r):
            for col in range(2):
                pad[1 + col, 1 + r] = t32[
                    pl.ds(col * rows + r, nz, stride=cells)
                ].astype(BF16)

    def halo(which, pad, act):
        for at, (dr, dc) in enumerate(SIDES):
            there = (-dr, -dc)
            from_rows = {-1: pl.ds(1, 1), 0: pl.ds(1, rows), 1: pl.ds(rows, 1)}[dr]
            to_rows = {-1: pl.ds(rows + 1, 1), 0: pl.ds(1, rows), 1: pl.ds(0, 1)}[dr]
            from_cols = {-1: pl.ds(1, 1), 0: pl.ds(1, 2), 1: pl.ds(2, 1)}[dc]
            to_cols = {-1: pl.ds(3, 1), 0: pl.ds(1, 2), 1: pl.ds(0, 1)}[dc]
            copy = pltpu.make_async_remote_copy(
                pad.at[from_cols, from_rows], pad.at[to_cols, to_rows],
                halo_send.at[which, at], halo_recv.at[which, at],
                device_id=beside(dr, dc), device_id_type=MESH,
            )
            if act == "send":
                pl.when(here(dr, dc))(copy.start)
            elif act == "sent":
                pl.when(here(dr, dc))(copy.wait_send)
            else:
                pl.when(here(*there))(copy.wait_recv)

    def lay_out(pad, cols, flip):
        for tap, (di, dj) in enumerate(TAPS):
            a, b = (2 - di, 2 - dj) if flip else (di, dj)
            cols[:, tap * ln : (tap + 1) * ln] = pad[b : b + 2, a : a + rows].reshape(block, ln)

    def carry_copy(send, recv, which, to):
        return pltpu.make_async_remote_copy(
            send, recv.at[x], car_send.at[which, to], car_recv.at[which, x],
            device_id=(to * nz + z, y, c), device_id_type=MESH,
        )

    def carry_from(recv, which, source):
        return pltpu.make_async_copy(recv.at[source], recv.at[source], car_recv.at[which, source])

    def fold(recv, which, order, needed):
        entry[...] = jnp.zeros_like(entry)
        for source in order:
            @pl.when(needed(source))
            def _():
                carry_from(recv, which, source).wait()
                for h in range(2):
                    entry[h] = (
                        recv[source, h, :cells] + recv[source, h, cells : cells + 1] * entry[h]
                    )

    frame = lambda t: pl.ds(t, cells, stride=nz)

    arrived(1, recv_c)
    unpack(recv_c, pad_c)
    halo(0, pad_c, "send")
    arrived(2, recv_i)
    unpack(recv_i, pad_i)
    halo(1, pad_i, "send")
    halo(0, pad_c, "arrive")
    lay_out(pad_c, cols_c, True)
    value = dot(cols_c[...], w_exc[...], ((1,), (0,)))
    exc[0] = value[:, :ln]
    exc[1] = value[:, ln:]

    for h in range(2):
        def adjoint_step(i, held):
            b, factor = held
            t = nz - 1 - i
            rate = decp[h, pl.ds(t, 1)]
            return rate * (exc[h, frame(t)] + b), factor * rate

        b, factor = lax.fori_loop(
            0, nz, adjoint_step, (jnp.zeros((cells, ln), F32), jnp.ones((1, ln), F32))
        )
        carry_a[h, :cells] = b
        carry_a[h, cells:] = jnp.broadcast_to(factor, (8, ln))
    for to in range(nx):
        pl.when(to < x)(carry_copy(carry_a, carries_a, 0, to).start)


    halo(1, pad_i, "arrive")
    lay_out(pad_i, cols_i, False)
    value = dot(cols_i[...], w_src[...], ((1,), (0,)))
    src[0] = value[:, :ln]
    src[1] = value[:, ln:]
    for h in range(2):
        def state_step(t, level):
            return decp[h, pl.ds(t, 1)] * level + src[h, frame(t)]

        carry_s[h, :cells] = lax.fori_loop(0, nz, state_step, jnp.zeros((cells, ln), F32))
        carry_s[h, cells:] = carry_a[h, cells:]
    for to in range(nx):
        pl.when(to > x)(carry_copy(carry_s, carries_s, 1, to).start)

    fold(carries_a, 0, range(nx - 1, -1, -1), lambda source: source > x)
    for h in range(2):
        def adjoint_final(i, b):
            t = nz - 1 - i
            level = exc[h, frame(t)] + b
            exc[h, frame(t)] = level
            return decp[h, pl.ds(t, 1)] * level

        lax.fori_loop(0, nz, adjoint_final, entry[h])
    adjoint_b = jnp.concatenate([exc[0], exc[1]], axis=1).astype(BF16)
    pad_a[1:3, 1 : 1 + rows] = adjoint_b.reshape(2, rows, nz, states)
    halo(2, pad_a, "send")

    def core_copy():
        return pltpu.make_async_remote_copy(
            grad_b, from_core, core_sem.at[0], core_sem.at[1],
            device_id=(tm, y, 1 - c), device_id_type=MESH,
        )

    grad[0] = dot(
        pad_a[1:3, 1 : 1 + rows].reshape(block, states), cols_i[...], ((0,), (0,))
    ).reshape(grad.shape[1:])

    def xy_copy(o):
        to = (flat + o) % (nx * ny)
        return pltpu.make_async_remote_copy(
            part_b.at[to % ny, to // ny], from_xy.at[o - 1], xy_send.at[o - 1], xy_recv.at[o - 1],
            device_id=flat_id(o), device_id_type=MESH,
        )

    def begin():
        core_copy().wait_recv()
        part_b[...] = (grad[c] + from_core[...].astype(F32)).astype(BF16)

        @pl.loop(1, nx * ny)
        def _(o):
            xy_copy(o).start()

    @pl.when(c == 1)
    def _():
        grad_b[...] = grad[0].astype(BF16)
        core_copy().start()

    fold(carries_s, 1, range(nx), lambda source: source < x)
    for h in range(2):
        def state_final(t, level):
            now = decp[h, pl.ds(t, 1)] * level + src[h, frame(t)]
            src[h, frame(t)] = now
            dg_part[h, pl.ds(t, 1)] = jnp.sum(exc[h, frame(t)] * level, axis=0, keepdims=True)
            return now

        lax.fori_loop(0, nz, state_final, entry[h])
    state_b = jnp.concatenate([src[0], src[1]], axis=1).astype(BF16)
    grad[1] = dot(state_b, cols_c[...], ((0,), (0,))).reshape(grad.shape[1:])

    @pl.when(c == 0)
    def _():
        grad_b[...] = grad[1].astype(BF16)
        core_copy().start()

    begin()

    halo(2, pad_a, "arrive")
    total = skip_ref[...] * pad_c[1:3, 1 : 1 + rows].reshape(block, ln).astype(F32)
    for tap, (di, dj) in enumerate(TAPS):
        a, b = 2 - di, 2 - dj
        total += dot(pad_a[b : b + 2, a : a + rows].reshape(block, states), w_back[tap], ((1,), (0,)))
    t32[...] = total

    @pl.loop(0, nz)
    def _(t):
        send_d[t] = t32[frame(t)].astype(BF16)

    give_back(3, send_d, recv_d)

    dg_old = exact_dot(
        jnp.concatenate([dg_part[0], dg_part[1]], axis=1), perm, ((1,), (1,))
    )
    high = dg_old.astype(BF16).astype(F32)
    mid = (dg_old - high).astype(BF16).astype(F32)
    low = dg_old - high - mid
    mail32[:, 15] = jnp.zeros((nz, ln), F32)
    for at, part in enumerate((high, mid, low)):
        mail32[:, 9 + 2 * at] = part[:, :ln]
        mail32[:, 10 + 2 * at] = part[:, ln:]

    def xy_sum(o, total):
        xy_copy(o).wait_recv()
        return total + from_xy[o - 1].astype(F32)

    summed = lax.fori_loop(1, nx * ny, xy_sum, grad[c, y, x] + from_core[y, x].astype(F32))
    for tap in range(9):
        mail32[:, tap] = summed[:, tap * ln : (tap + 1) * ln]
    mail[...] = mail32[...].astype(BF16)

    give_back(4, mail, from_z)

    arrived(3, recv_d)
    t32[...] = recv_d[...].astype(F32).reshape(block, ln)

    @pl.loop(0, rows)
    def _(r):
        dinp_ref[r] = t32[pl.ds(r, wide, stride=rows)].astype(BF16)

    put_dinp = pltpu.make_async_copy(dinp_ref, dinp_hbm, put_sem.at[0])
    put_dinp.start()

    arrived(4, from_z)
    both = [jnp.zeros((16, ln), F32), jnp.zeros((16, ln), F32)]
    for k in range(nz):
        both[k % 2] = both[k % 2] + from_z[k].astype(F32)
    share[:9] = both[0][:9]
    share[9:18] = both[1][:9]
    rest = both[0] + both[1]
    share[18:20] = rest[9:11] + (rest[11:13] + rest[13:15])

    def share_copy(o):
        return pltpu.make_async_remote_copy(
            share, shares.at[spot], ag_send.at[o - 1], ag_recv.at[o - 1],
            device_id=spot_id(o), device_id_type=MESH,
        )

    for o in range(1, 2 * ny):
        share_copy(o).start()
    own = pltpu.make_async_copy(share, shares.at[spot], put_sem.at[1])
    own.start()
    for o in range(1, 2 * ny):
        share_copy(o).wait_recv()
    own.wait()
    put_dinp.wait()

    sent(0, dec_in)
    sent(1, send_c)
    sent(2, send_i)
    sent(3, send_d)
    sent(4, mail)
    for which, pad in enumerate((pad_c, pad_i, pad_a)):
        halo(which, pad, "sent")
    for to in range(nx):
        pl.when(to < x)(carry_copy(carry_a, carries_a, 0, to).wait_send)
        pl.when(to > x)(carry_copy(carry_s, carries_s, 1, to).wait_send)
    core_copy().wait_send()

    @pl.loop(1, nx * ny)
    def _(o):
        xy_copy(o).wait_send()

    for o in range(1, 2 * ny):
        share_copy(o).wait_send()


def finish(ny, ln, wscale, dscale, dinp_hbm, shares_hbm, out_hbm, din_ref, dout_ref, dg_ref, shares, tile, sem):
    fetch = pltpu.make_async_copy(shares_hbm, shares, sem.at[0])
    come = pltpu.make_async_copy(dinp_hbm, tile, sem.at[1])
    go = pltpu.make_async_copy(tile, out_hbm, sem.at[2])
    come.start()
    fetch.start()
    come.wait()
    go.start()
    fetch.wait()
    for j in range(ny):
        both = shares[2 * j] + shares[2 * j + 1]
        din_ref[:, j] = both[:9] * wscale
        dout_ref[:, j] = both[9:18] * wscale
    total = shares[0, 18:20]
    for s in range(1, 2 * ny):
        total += shares[s, 18:20]
    dg_ref[:, :ln] = total[:1] * dscale
    dg_ref[:, ln:] = total[1:] * dscale
    go.wait()


def body(nx, inputs, cotangent, w_in, w_out, decay, skip):
    _, rows, wide, ln = inputs.shape
    ny = lax.axis_size("row")
    nz = lax.axis_size("tm") // nx
    states = w_in.shape[3]
    cells = 2 * rows
    block = cells * nz
    wscale = 1.0 / math.sqrt(nx * nz * ny * rows * wide * 2)
    dscale = 1.0 / math.sqrt(ny * rows * wide * 2)
    vmem = pltpu.VMEM
    dma = pltpu.SemaphoreType.DMA
    scratch = [
        vmem((rows, wide, ln), BF16),
        vmem((rows, wide, ln), BF16),
        vmem((9, ln, states), BF16),
        vmem((9, states, ln), BF16),
        vmem((1, states), F32),
        vmem((1, ln), F32),
        dma((6,)),
        vmem((block, ln), F32),
        vmem((nz, cells, ln), BF16),
        vmem((nz, cells, ln), BF16),
        vmem((nz, cells, ln), BF16),
        vmem((nz, cells, ln), BF16),
        vmem((nz, cells, ln), BF16),
        vmem((nz, cells, ln), BF16),
        vmem((nz, 1, states), F32),
        vmem((2, nz, ln), F32),
        vmem((4, rows + 2, nz, ln), BF16),
        vmem((4, rows + 2, nz, ln), BF16),
        vmem((4, rows + 2, nz, states), BF16),
        vmem((block, 9 * ln), BF16),
        vmem((block, 9 * ln), BF16),
        vmem((9 * ln, states), BF16),
        vmem((9 * ln, states), BF16),
        vmem((9, states, ln), BF16),
        vmem((2, block, ln), F32),
        vmem((2, block, ln), F32),
        vmem((2, cells + 8, ln), F32),
        vmem((nx, 2, cells + 8, ln), F32),
        vmem((2, cells + 8, ln), F32),
        vmem((nx, 2, cells + 8, ln), F32),
        vmem((2, cells, ln), F32),
        vmem((2, nz, ln), F32),
        vmem((2, ny, nx, nz, 9 * ln), F32),
        vmem((ny, nx, nz, 9 * ln), BF16),
        vmem((ny, nx, nz, 9 * ln), BF16),
        vmem((ny, nx, nz, 9 * ln), BF16),
        vmem((nx * ny - 1, nz, 9 * ln), BF16),
        vmem((nz, 16, ln), F32),
        vmem((nz, 16, ln), BF16),
        vmem((nz, 16, ln), BF16),
        vmem((20, ln), F32),
        vmem((rows, wide, ln), BF16),
        dma((2,)),
        dma((5,)),
        dma((5,)),
        dma((3, 8)),
        dma((3, 8)),
        dma((2, nx)),
        dma((2, nx)),
        dma((2,)),
        dma((nx * ny - 1,)),
        dma((nx * ny - 1,)),
        dma((2 * ny - 1,)),
        dma((2 * ny - 1,)),
    ]
    tile = jax.ShapeDtypeStruct((rows, wide, ln), BF16)
    d_inputs, shares = pl.pallas_call(
        functools.partial(kernel, nx, nz, ny, rows, ln),
        out_shape=(tile, jax.ShapeDtypeStruct((2 * ny, 20, ln), F32)),
        in_specs=[pl.BlockSpec(memory_space=pltpu.HBM)] * 6,
        out_specs=(pl.BlockSpec(memory_space=pltpu.HBM), pl.BlockSpec(memory_space=pltpu.HBM)),
        scratch_shapes=scratch,
        compiler_params=pltpu.CompilerParams(
            collective_id=0, has_side_effects=True, vmem_limit_bytes=63 * 1024 * 1024
        ),
        cost_estimate=pl.CostEstimate(
            flops=5 * 2 * block * 9 * ln * states, bytes_accessed=4 * 1024 * 1024, transcendentals=0
        ),
    )(
        inputs.reshape(rows, wide, ln),
        cotangent.reshape(rows, wide, ln),
        w_in.reshape(9, ln, states),
        w_out.reshape(9, states, ln),
        decay,
        skip.reshape(1, ln),
    )
    whole = pl.BlockSpec(memory_space=pltpu.VMEM)
    d_inputs, d_in, d_out, d_decay = pl.pallas_call(
        functools.partial(finish, ny, ln, wscale, dscale),
        out_shape=(
            tile,
            jax.ShapeDtypeStruct((9, ny, ln), F32),
            jax.ShapeDtypeStruct((9, ny, ln), F32),
            jax.ShapeDtypeStruct((1, states), F32),
        ),
        in_specs=[pl.BlockSpec(memory_space=pltpu.HBM)] * 2,
        out_specs=(pl.BlockSpec(memory_space=pltpu.HBM), whole, whole, whole),
        scratch_shapes=[vmem((2 * ny, 20, ln), F32), vmem((rows, wide, ln), BF16), dma((3,))],
        compiler_params=pltpu.CompilerParams(vmem_limit_bytes=63 * 1024 * 1024),
    )(d_inputs, shares)

    def by_channel(grad):
        return jnp.transpose(grad.reshape(3, 3, ny, ln), (2, 0, 1, 3))

    return (d_inputs[None], by_channel(d_in), by_channel(d_out), d_decay)


def solution(mesh, nx=X_CHIPS):
    in_specs = (
        P("tm", "row", "col", None),
        P("tm", "row", "col", None),
        P(),
        P(),
        P("tm", None),
        P(),
    )
    out_specs = (
        P("tm", "row", "col", None),
        P("tm", None, None, None),
        P("tm", None, None, None),
        P("tm", None),
    )
    return jax.shard_map(
        functools.partial(body, nx), mesh=mesh, in_specs=in_specs, out_specs=out_specs,
        check_vma=False,
    )
```

```python
import functools
import math

import jax
import jax.numpy as jnp
from jax import lax
from jax.experimental import pallas as pl
from jax.experimental.pallas import tpu as pltpu
from jax.sharding import PartitionSpec as P

MESH = pl.DeviceIdType.MESH
F32 = jnp.float32
BF16 = jnp.bfloat16
X_CHIPS = 4
TAPS = [(di, dj) for di in range(3) for dj in range(3)]
SIDES = [(dr, dc) for dr in (-1, 0, 1) for dc in (-1, 0, 1) if dr or dc]


def dot(a, b, dims):
    return lax.dot_general(a, b, (dims, ((), ())), preferred_element_type=F32)


def exact_dot(a, b, dims):
    high = a.astype(BF16)
    rest = a - high.astype(F32)
    mid = rest.astype(BF16)
    low = (rest - mid.astype(F32)).astype(BF16)
    return dot(high, b, dims) + dot(mid, b, dims) + dot(low, b, dims)


def kernel(
    nx, nz, ny, rows, ln,
    in_hbm, cot_hbm, win_hbm, wout_hbm, dec_hbm, skip_hbm,
    dinp_hbm, shares,
    in_ref, cot_ref, win_ref, wout_ref, dec_ref, skip_ref, fetch_sem,
    t32, send_c, send_i, send_d, recv_c, recv_i, recv_d, dec_in, decp,
    pad_c, pad_i, pad_a, cols_c, cols_i, w_src, w_exc, w_back,
    exc, src,
    carry_a, carries_a, carry_s, carries_s, entry, dg_part,
    grad, grad_b, from_core, part_b, from_xy,
    mail32, mail, from_z, share, dinp_ref, put_sem,
    p1_send, p1_recv, halo_send, halo_recv, car_send, car_recv,
    core_send, core_recv, xy_send, xy_recv, ag_send, ag_recv,
):
    cells = 2 * rows
    wide = 2 * nz
    states = 2 * ln
    block = cells * nz
    tm = lax.axis_index("tm")
    y = lax.axis_index("row")
    c = lax.axis_index("col")
    x = tm // nz
    z = tm % nz
    q = 2 * z + c
    home = q // nz
    place = q % nz
    paired = home == c
    spot = 2 * y + c
    flat = x * ny + y

    def here(dr, dc):
        return (y + dr >= 0) & (y + dr < ny) & (q + dc >= 0) & (q + dc < wide)

    def beside(dr, dc):
        to = q + dc
        return (x * nz + to // 2, y + dr, to % 2)

    def flat_id(o):
        to = (flat + o) % (nx * ny)
        return ((to // ny) * nz + z, to % ny, c)

    def spot_id(o):
        to = (spot + o) % (2 * ny)
        return (tm, to // 2, to % 2)

    def chip(i):
        odd = i % 2
        return (z + nz // 2 + (1 - odd) * (i // 2) - odd * ((i + 1) // 2) + nz) % nz

    fetches = [
        pltpu.make_async_copy(source, target, fetch_sem.at[at])
        for at, (source, target) in enumerate([
            (cot_hbm, cot_ref), (in_hbm, in_ref), (dec_hbm, dec_ref),
            (wout_hbm, wout_ref), (win_hbm, win_ref), (skip_hbm, skip_ref),
        ])
    ]
    for fetch in fetches:
        fetch.start()

    barrier = pltpu.get_barrier_semaphore()

    def greet(device):
        pl.semaphore_signal(barrier, inc=1, device_id=device, device_id_type=MESH)

    @pl.loop(0, nz)
    def _(i):
        t = chip(i)

        @pl.when(jnp.logical_not(paired & (t == z)))
        def _():
            greet((x * nz + t, y, home))

    @pl.loop(1, nx * ny)
    def _(o):
        greet(flat_id(o))

    for o in range(1, 2 * ny, 2):
        greet((tm, (y + o // 2) % ny, 1 - c))

    pad_c[...] = jnp.zeros_like(pad_c)
    pad_i[...] = jnp.zeros_like(pad_i)
    pad_a[...] = jnp.zeros_like(pad_a)

    beside_count = jnp.int32(0)
    for dr, dc in SIDES:
        beside_count += here(dr, dc).astype(jnp.int32)

        @pl.when(here(dr, dc))
        def _():
            greet(beside(dr, dc))


    def pack(ref, out):
        t32[...] = ref[...].astype(F32).reshape(block, ln)

        @pl.loop(0, nz)
        def _(k):
            for col in range(2):
                out[k, col * rows : (col + 1) * rows] = t32[
                    pl.ds(2 * k + col, rows, stride=wide)
                ].astype(BF16)

    def scatter(at, source, target):
        @pl.loop(0, nz)
        def _(i):
            to = chip(i)
            for core in range(2):
                k = 2 * to + core - c * nz
                wanted = (k >= 0) & (k < nz)
                own = (to == z) & (c == core)

                @pl.when(wanted & own)
                def _():
                    pltpu.make_async_copy(source(k), target.at[z], p1_recv.at[at]).start()

                @pl.when(wanted & jnp.logical_not(own))
                def _():
                    pltpu.make_async_remote_copy(
                        source(k), target.at[z], p1_send.at[at], p1_recv.at[at],
                        device_id=(x * nz + to, y, core), device_id_type=MESH,
                    ).start()

    def give_back(at, source, target):
        @pl.loop(0, nz)
        def _(i):
            t = chip(i)
            own = paired & (t == z)

            @pl.when(own)
            def _():
                pltpu.make_async_copy(source.at[t], target.at[place], p1_recv.at[at]).start()

            @pl.when(jnp.logical_not(own))
            def _():
                pltpu.make_async_remote_copy(
                    source.at[t], target.at[place], p1_send.at[at], p1_recv.at[at],
                    device_id=(x * nz + t, y, home), device_id_type=MESH,
                ).start()

    def arrived(at, target):
        pltpu.make_async_copy(target, target, p1_recv.at[at]).wait()

    def sent(at, like):
        @pl.when(paired)
        def _():
            part = like.at[pl.ds(0, nz - 1)]
            pltpu.make_async_copy(part, part, p1_send.at[at]).wait()

        @pl.when(jnp.logical_not(paired))
        def _():
            pltpu.make_async_copy(like, like, p1_send.at[at]).wait()

    fetches[0].wait()
    pack(cot_ref, send_c)
    pl.semaphore_wait(
        barrier, nz - paired.astype(jnp.int32) + beside_count + (nx * ny - 1) + ny
    )
    scatter(1, lambda k: send_c.at[k], recv_c)
    fetches[1].wait()
    pack(in_ref, send_i)
    fetches[2].wait()
    scatter(0, lambda k: dec_ref, dec_in)
    scatter(2, lambda k: send_i.at[k], recv_i)
    fetches[3].wait()
    fetches[4].wait()
    fetches[5].wait()

    old = lax.broadcasted_iota(jnp.int32, (states, states), 0)
    new = lax.broadcasted_iota(jnp.int32, (states, states), 1)
    perm = jnp.where((old % ny) * (nx * nz) + old // ny == new, 1.0, 0.0).astype(BF16)

    @pl.loop(0, 9)
    def _(tap):
        at = pl.ds(pl.multiple_of(tap * ln, ln), ln)
        w_src[at] = dot(win_ref[tap], perm, ((1,), (0,))).astype(BF16)
        w_exc[at] = dot(wout_ref[tap], perm, ((0,), (0,))).astype(BF16)
        w_back[tap] = dot(perm, win_ref[tap], ((0,), (1,))).astype(BF16)

    arrived(0, dec_in)
    rates = exact_dot(dec_in[...].reshape(nz, states), perm, ((1,), (0,)))
    decp[0] = rates[:, :ln]
    decp[1] = rates[:, ln:]

    def unpack(recv, pad):
        t32[...] = recv[...].astype(F32).reshape(block, ln)

        @pl.loop(0, rows)
        def _(r):
            for col in range(2):
                pad[1 + col, 1 + r] = t32[
                    pl.ds(col * rows + r, nz, stride=cells)
                ].astype(BF16)

    def halo(which, pad, act):
        for at, (dr, dc) in enumerate(SIDES):
            there = (-dr, -dc)
            from_rows = {-1: pl.ds(1, 1), 0: pl.ds(1, rows), 1: pl.ds(rows, 1)}[dr]
            to_rows = {-1: pl.ds(rows + 1, 1), 0: pl.ds(1, rows), 1: pl.ds(0, 1)}[dr]
            from_cols = {-1: pl.ds(1, 1), 0: pl.ds(1, 2), 1: pl.ds(2, 1)}[dc]
            to_cols = {-1: pl.ds(3, 1), 0: pl.ds(1, 2), 1: pl.ds(0, 1)}[dc]
            copy = pltpu.make_async_remote_copy(
                pad.at[from_cols, from_rows], pad.at[to_cols, to_rows],
                halo_send.at[which, at], halo_recv.at[which, at],
                device_id=beside(dr, dc), device_id_type=MESH,
            )
            if act == "send":
                pl.when(here(dr, dc))(copy.start)
            elif act == "sent":
                pl.when(here(dr, dc))(copy.wait_send)
            else:
                pl.when(here(*there))(copy.wait_recv)

    def lay_out(pad, cols, flip):
        for tap, (di, dj) in enumerate(TAPS):
            a, b = (2 - di, 2 - dj) if flip else (di, dj)
            cols[:, tap * ln : (tap + 1) * ln] = pad[b : b + 2, a : a + rows].reshape(block, ln)

    def carry_copy(send, recv, which, to):
        return pltpu.make_async_remote_copy(
            send, recv.at[x], car_send.at[which, to], car_recv.at[which, x],
            device_id=(to * nz + z, y, c), device_id_type=MESH,
        )

    def carry_from(recv, which, source):
        return pltpu.make_async_copy(recv.at[source], recv.at[source], car_recv.at[which, source])

    def fold(recv, which, order, needed):
        entry[...] = jnp.zeros_like(entry)
        for source in order:
            @pl.when(needed(source))
            def _():
                carry_from(recv, which, source).wait()
                for h in range(2):
                    entry[h] = (
                        recv[source, h, :cells] + recv[source, h, cells : cells + 1] * entry[h]
                    )

    frame = lambda t: pl.ds(t, cells, stride=nz)

    arrived(1, recv_c)
    unpack(recv_c, pad_c)
    halo(0, pad_c, "send")
    arrived(2, recv_i)
    unpack(recv_i, pad_i)
    halo(1, pad_i, "send")
    halo(0, pad_c, "arrive")
    lay_out(pad_c, cols_c, True)
    value = dot(cols_c[...], w_exc[...], ((1,), (0,)))
    exc[0] = value[:, :ln]
    exc[1] = value[:, ln:]

    for h in range(2):
        def adjoint_step(i, held):
            b, factor = held
            t = nz - 1 - i
            rate = decp[h, pl.ds(t, 1)]
            return rate * (exc[h, frame(t)] + b), factor * rate

        b, factor = lax.fori_loop(
            0, nz, adjoint_step, (jnp.zeros((cells, ln), F32), jnp.ones((1, ln), F32))
        )
        carry_a[h, :cells] = b
        carry_a[h, cells:] = jnp.broadcast_to(factor, (8, ln))
    for to in range(nx):
        pl.when(to < x)(carry_copy(carry_a, carries_a, 0, to).start)

    halo(1, pad_i, "arrive")
    lay_out(pad_i, cols_i, False)
    value = dot(cols_i[...], w_src[...], ((1,), (0,)))
    src[0] = value[:, :ln]
    src[1] = value[:, ln:]
    for h in range(2):
        def state_step(t, level):
            return decp[h, pl.ds(t, 1)] * level + src[h, frame(t)]

        carry_s[h, :cells] = lax.fori_loop(0, nz, state_step, jnp.zeros((cells, ln), F32))
        carry_s[h, cells:] = carry_a[h, cells:]
    for to in range(nx):
        pl.when(to > x)(carry_copy(carry_s, carries_s, 1, to).start)

    fold(carries_a, 0, range(nx - 1, -1, -1), lambda source: source > x)
    for h in range(2):
        def adjoint_final(i, b):
            t = nz - 1 - i
            level = exc[h, frame(t)] + b
            exc[h, frame(t)] = level
            return decp[h, pl.ds(t, 1)] * level

        lax.fori_loop(0, nz, adjoint_final, entry[h])
    adjoint_b = jnp.concatenate([exc[0], exc[1]], axis=1).astype(BF16)
    pad_a[1:3, 1 : 1 + rows] = adjoint_b.reshape(2, rows, nz, states)
    halo(2, pad_a, "send")

    half = ny // 2

    def core_copy(h):
        part = pl.ds(h * half, half)
        return pltpu.make_async_remote_copy(
            grad_b.at[part], from_core.at[part], core_send.at[h], core_recv.at[h],
            device_id=(tm, y, 1 - c), device_id_type=MESH,
        )

    def xy_copy(o):
        to = (flat + o) % (nx * ny)
        return pltpu.make_async_remote_copy(
            part_b.at[to % ny, to // ny], from_xy.at[o - 1], xy_send.at[o - 1], xy_recv.at[o - 1],
            device_id=flat_id(o), device_id_type=MESH,
        )

    def gradient(which, h, levels, cols):
        part = slice(h * half, (h + 1) * half)
        value = dot(levels[h].astype(BF16), cols[...], ((0,), (0,)))
        grad[which, part] = value.reshape(half, nx, nz, 9 * ln)

        @pl.when(c != which)
        def _():
            grad_b[part] = grad[which, part].astype(BF16)
            core_copy(h).start()

    def begin():
        for h in range(2):
            core_copy(h).wait_recv()
            part = slice(h * half, (h + 1) * half)
            part_b[part] = (grad[c, part] + from_core[part].astype(F32)).astype(BF16)

            @pl.loop(1, nx * ny)
            def _(o):
                pl.when(((flat + o) % ny) // half == h)(lambda: xy_copy(o).start())

    for h in range(2):
        gradient(0, h, exc, cols_i)
    pl.when(c == 0)(begin)

    fold(carries_s, 1, range(nx), lambda source: source < x)
    for h in range(2):
        def state_final(t, level):
            now = decp[h, pl.ds(t, 1)] * level + src[h, frame(t)]
            src[h, frame(t)] = now
            dg_part[h, pl.ds(t, 1)] = jnp.sum(exc[h, frame(t)] * level, axis=0, keepdims=True)
            return now

        lax.fori_loop(0, nz, state_final, entry[h])
        gradient(1, h, src, cols_c)
    pl.when(c == 1)(begin)

    halo(2, pad_a, "arrive")
    total = skip_ref[...] * pad_c[1:3, 1 : 1 + rows].reshape(block, ln).astype(F32)
    for tap, (di, dj) in enumerate(TAPS):
        a, b = 2 - di, 2 - dj
        total += dot(pad_a[b : b + 2, a : a + rows].reshape(block, states), w_back[tap], ((1,), (0,)))
    t32[...] = total

    @pl.loop(0, nz)
    def _(t):
        send_d[t] = t32[frame(t)].astype(BF16)

    give_back(3, send_d, recv_d)

    dg_old = exact_dot(
        jnp.concatenate([dg_part[0], dg_part[1]], axis=1), perm, ((1,), (1,))
    )
    high = dg_old.astype(BF16).astype(F32)
    mid = (dg_old - high).astype(BF16).astype(F32)
    low = dg_old - high - mid
    mail32[:, 15] = jnp.zeros((nz, ln), F32)
    for at, part in enumerate((high, mid, low)):
        mail32[:, 9 + 2 * at] = part[:, :ln]
        mail32[:, 10 + 2 * at] = part[:, ln:]

    def xy_sum(o, total):
        xy_copy(o).wait_recv()
        return total + from_xy[o - 1].astype(F32)

    summed = lax.fori_loop(1, nx * ny, xy_sum, grad[c, y, x] + from_core[y, x].astype(F32))
    for tap in range(9):
        mail32[:, tap] = summed[:, tap * ln : (tap + 1) * ln]
    mail[...] = mail32[...].astype(BF16)

    give_back(4, mail, from_z)

    arrived(3, recv_d)
    t32[...] = recv_d[...].astype(F32).reshape(block, ln)

    @pl.loop(0, rows)
    def _(r):
        dinp_ref[r] = t32[pl.ds(r, wide, stride=rows)].astype(BF16)

    put_dinp = pltpu.make_async_copy(dinp_ref, dinp_hbm, put_sem.at[0])
    put_dinp.start()

    arrived(4, from_z)
    both = [jnp.zeros((16, ln), F32), jnp.zeros((16, ln), F32)]
    for k in range(nz):
        both[k % 2] = both[k % 2] + from_z[k].astype(F32)
    share[:9] = both[0][:9]
    share[9:18] = both[1][:9]
    rest = both[0] + both[1]
    share[18:20] = rest[9:11] + (rest[11:13] + rest[13:15])

    def share_copy(o):
        return pltpu.make_async_remote_copy(
            share, shares.at[spot], ag_send.at[o - 1], ag_recv.at[o - 1],
            device_id=spot_id(o), device_id_type=MESH,
        )

    for o in range(1, 2 * ny):
        share_copy(o).start()
    own = pltpu.make_async_copy(share, shares.at[spot], put_sem.at[1])
    own.start()
    for o in range(1, 2 * ny):
        share_copy(o).wait_recv()
    own.wait()
    put_dinp.wait()

    sent(0, dec_in)
    sent(1, send_c)
    sent(2, send_i)
    sent(3, send_d)
    sent(4, mail)
    for which, pad in enumerate((pad_c, pad_i, pad_a)):
        halo(which, pad, "sent")
    for to in range(nx):
        pl.when(to < x)(carry_copy(carry_a, carries_a, 0, to).wait_send)
        pl.when(to > x)(carry_copy(carry_s, carries_s, 1, to).wait_send)
    for h in range(2):
        core_copy(h).wait_send()

    @pl.loop(1, nx * ny)
    def _(o):
        xy_copy(o).wait_send()

    for o in range(1, 2 * ny):
        share_copy(o).wait_send()


def finish(ny, ln, wscale, dscale, dinp_hbm, shares_hbm, out_hbm, din_ref, dout_ref, dg_ref, shares, tile, sem):
    fetch = pltpu.make_async_copy(shares_hbm, shares, sem.at[0])
    come = pltpu.make_async_copy(dinp_hbm, tile, sem.at[1])
    go = pltpu.make_async_copy(tile, out_hbm, sem.at[2])
    come.start()
    fetch.start()
    come.wait()
    go.start()
    fetch.wait()
    for j in range(ny):
        both = shares[2 * j] + shares[2 * j + 1]
        din_ref[:, j] = both[:9] * wscale
        dout_ref[:, j] = both[9:18] * wscale
    total = shares[0, 18:20]
    for s in range(1, 2 * ny):
        total += shares[s, 18:20]
    dg_ref[:, :ln] = total[:1] * dscale
    dg_ref[:, ln:] = total[1:] * dscale
    go.wait()


def body(nx, inputs, cotangent, w_in, w_out, decay, skip):
    _, rows, wide, ln = inputs.shape
    ny = lax.axis_size("row")
    nz = lax.axis_size("tm") // nx
    states = w_in.shape[3]
    cells = 2 * rows
    block = cells * nz
    wscale = 1.0 / math.sqrt(nx * nz * ny * rows * wide * 2)
    dscale = 1.0 / math.sqrt(ny * rows * wide * 2)
    vmem = pltpu.VMEM
    dma = pltpu.SemaphoreType.DMA
    scratch = [
        vmem((rows, wide, ln), BF16),
        vmem((rows, wide, ln), BF16),
        vmem((9, ln, states), BF16),
        vmem((9, states, ln), BF16),
        vmem((1, states), F32),
        vmem((1, ln), F32),
        dma((6,)),
        vmem((block, ln), F32),
        vmem((nz, cells, ln), BF16),
        vmem((nz, cells, ln), BF16),
        vmem((nz, cells, ln), BF16),
        vmem((nz, cells, ln), BF16),
        vmem((nz, cells, ln), BF16),
        vmem((nz, cells, ln), BF16),
        vmem((nz, 1, states), F32),
        vmem((2, nz, ln), F32),
        vmem((4, rows + 2, nz, ln), BF16),
        vmem((4, rows + 2, nz, ln), BF16),
        vmem((4, rows + 2, nz, states), BF16),
        vmem((block, 9 * ln), BF16),
        vmem((block, 9 * ln), BF16),
        vmem((9 * ln, states), BF16),
        vmem((9 * ln, states), BF16),
        vmem((9, states, ln), BF16),
        vmem((2, block, ln), F32),
        vmem((2, block, ln), F32),
        vmem((2, cells + 8, ln), F32),
        vmem((nx, 2, cells + 8, ln), F32),
        vmem((2, cells + 8, ln), F32),
        vmem((nx, 2, cells + 8, ln), F32),
        vmem((2, cells, ln), F32),
        vmem((2, nz, ln), F32),
        vmem((2, ny, nx, nz, 9 * ln), F32),
        vmem((ny, nx, nz, 9 * ln), BF16),
        vmem((ny, nx, nz, 9 * ln), BF16),
        vmem((ny, nx, nz, 9 * ln), BF16),
        vmem((nx * ny - 1, nz, 9 * ln), BF16),
        vmem((nz, 16, ln), F32),
        vmem((nz, 16, ln), BF16),
        vmem((nz, 16, ln), BF16),
        vmem((20, ln), F32),
        vmem((rows, wide, ln), BF16),
        dma((2,)),
        dma((5,)),
        dma((5,)),
        dma((3, 8)),
        dma((3, 8)),
        dma((2, nx)),
        dma((2, nx)),
        dma((2,)),
        dma((2,)),
        dma((nx * ny - 1,)),
        dma((nx * ny - 1,)),
        dma((2 * ny - 1,)),
        dma((2 * ny - 1,)),
    ]
    tile = jax.ShapeDtypeStruct((rows, wide, ln), BF16)
    d_inputs, shares = pl.pallas_call(
        functools.partial(kernel, nx, nz, ny, rows, ln),
        out_shape=(tile, jax.ShapeDtypeStruct((2 * ny, 20, ln), F32)),
        in_specs=[pl.BlockSpec(memory_space=pltpu.HBM)] * 6,
        out_specs=(pl.BlockSpec(memory_space=pltpu.HBM), pl.BlockSpec(memory_space=pltpu.HBM)),
        scratch_shapes=scratch,
        compiler_params=pltpu.CompilerParams(
            collective_id=0, has_side_effects=True, vmem_limit_bytes=63 * 1024 * 1024
        ),
        cost_estimate=pl.CostEstimate(
            flops=5 * 2 * block * 9 * ln * states, bytes_accessed=4 * 1024 * 1024, transcendentals=0
        ),
    )(
        inputs.reshape(rows, wide, ln),
        cotangent.reshape(rows, wide, ln),
        w_in.reshape(9, ln, states),
        w_out.reshape(9, states, ln),
        decay,
        skip.reshape(1, ln),
    )
    whole = pl.BlockSpec(memory_space=pltpu.VMEM)
    d_inputs, d_in, d_out, d_decay = pl.pallas_call(
        functools.partial(finish, ny, ln, wscale, dscale),
        out_shape=(
            tile,
            jax.ShapeDtypeStruct((9, ny, ln), F32),
            jax.ShapeDtypeStruct((9, ny, ln), F32),
            jax.ShapeDtypeStruct((1, states), F32),
        ),
        in_specs=[pl.BlockSpec(memory_space=pltpu.HBM)] * 2,
        out_specs=(pl.BlockSpec(memory_space=pltpu.HBM), whole, whole, whole),
        scratch_shapes=[vmem((2 * ny, 20, ln), F32), vmem((rows, wide, ln), BF16), dma((3,))],
        compiler_params=pltpu.CompilerParams(vmem_limit_bytes=63 * 1024 * 1024),
    )(d_inputs, shares)

    def by_channel(grad):
        return jnp.transpose(grad.reshape(3, 3, ny, ln), (2, 0, 1, 3))

    return (d_inputs[None], by_channel(d_in), by_channel(d_out), d_decay)


def solution(mesh, nx=X_CHIPS):
    in_specs = (
        P("tm", "row", "col", None),
        P("tm", "row", "col", None),
        P(),
        P(),
        P("tm", None),
        P(),
    )
    out_specs = (
        P("tm", "row", "col", None),
        P("tm", None, None, None),
        P("tm", None, None, None),
        P("tm", None),
    )
    return jax.shard_map(
        functools.partial(body, nx), mesh=mesh, in_specs=in_specs, out_specs=out_specs,
        check_vma=False,
    )
```

```python
import functools
import math

import jax
import jax.numpy as jnp
from jax import lax
from jax.experimental import pallas as pl
from jax.experimental.pallas import tpu as pltpu
from jax.sharding import PartitionSpec as P

MESH = pl.DeviceIdType.MESH
F32 = jnp.float32
BF16 = jnp.bfloat16
X_CHIPS = 4
TAPS = [(di, dj) for di in range(3) for dj in range(3)]
SIDES = [(0, -1), (0, 1), (-1, -1), (1, 1), (-1, 1), (1, -1), (-1, 0), (1, 0)]


def far(i, n):
    odd = i % 2
    return n // 2 + (1 - odd) * (i // 2) - odd * ((i + 1) // 2)


def dot(a, b, dims):
    return lax.dot_general(a, b, (dims, ((), ())), preferred_element_type=F32)


def exact_dot(a, b, dims):
    high = a.astype(BF16)
    rest = a - high.astype(F32)
    mid = rest.astype(BF16)
    low = (rest - mid.astype(F32)).astype(BF16)
    return dot(high, b, dims) + dot(mid, b, dims) + dot(low, b, dims)


def kernel(
    nx, nz, ny, rows, ln,
    in_hbm, cot_hbm, win_hbm, wout_hbm, dec_hbm, skip_hbm,
    dinp_hbm, shares,
    in_ref, cot_ref, win_ref, wout_ref, dec_ref, skip_ref, fetch_sem,
    t32, send_c, send_i, send_d, recv_c, recv_i, recv_d, dec_in, decp,
    pad_c, pad_i, pad_a, cols_c, cols_i, w_src, w_exc, w_back,
    exc, src,
    carry_a, carries_a, carry_s, carries_s, entry, dg_part,
    grad, grad_b, from_core, part_b, from_xy,
    mail32, mail, from_z, share, dinp_ref, put_sem,
    p1_send, p1_recv, halo_send, halo_recv, car_send, car_recv,
    core_send, core_recv, xy_send, xy_recv, ag_send, ag_recv,
):
    cells = 2 * rows
    wide = 2 * nz
    states = 2 * ln
    block = cells * nz
    tm = lax.axis_index("tm")
    y = lax.axis_index("row")
    c = lax.axis_index("col")
    x = tm // nz
    z = tm % nz
    q = 2 * z + c
    home = q // nz
    place = q % nz
    paired = home == c
    spot = 2 * y + c

    def here(dr, dc):
        return (y + dr >= 0) & (y + dr < ny) & (q + dc >= 0) & (q + dc < wide)

    def beside(dr, dc):
        to = q + dc
        return (x * nz + to // 2, y + dr, to % 2)

    def flat_to(i):
        return (x + far(i // ny, nx)) % nx, (y + far(i % ny, ny)) % ny

    def flat_id(i):
        to_x, to_y = flat_to(i)
        return (to_x * nz + z, to_y, c)

    def spot_id(o):
        to = (spot + o) % (2 * ny)
        return (tm, to // 2, to % 2)

    def chip(i):
        return (z + far(i, nz)) % nz

    fetches = [
        pltpu.make_async_copy(source, target, fetch_sem.at[at])
        for at, (source, target) in enumerate([
            (cot_hbm, cot_ref), (in_hbm, in_ref), (dec_hbm, dec_ref),
            (wout_hbm, wout_ref), (win_hbm, win_ref), (skip_hbm, skip_ref),
        ])
    ]
    for fetch in fetches:
        fetch.start()

    barrier = pltpu.get_barrier_semaphore()

    def greet(device):
        pl.semaphore_signal(barrier, inc=1, device_id=device, device_id_type=MESH)

    @pl.loop(0, nz)
    def _(i):
        t = chip(i)

        @pl.when(jnp.logical_not(paired & (t == z)))
        def _():
            greet((x * nz + t, y, home))

    others = nx * ny - 1

    @pl.loop(0, others)
    def _(i):
        greet(flat_id(i))

    for o in range(1, 2 * ny, 2):
        greet((tm, (y + o // 2) % ny, 1 - c))

    pad_c[...] = jnp.zeros_like(pad_c)
    pad_i[...] = jnp.zeros_like(pad_i)
    pad_a[...] = jnp.zeros_like(pad_a)

    beside_count = jnp.int32(0)
    for dr, dc in SIDES:
        beside_count += here(dr, dc).astype(jnp.int32)

        @pl.when(here(dr, dc))
        def _():
            greet(beside(dr, dc))


    def pack(ref, out):
        t32[...] = ref[...].astype(F32).reshape(block, ln)

        @pl.loop(0, nz)
        def _(k):
            for col in range(2):
                out[k, col * rows : (col + 1) * rows] = t32[
                    pl.ds(2 * k + col, rows, stride=wide)
                ].astype(BF16)

    def scatter(at, source, target):
        @pl.loop(0, nz)
        def _(i):
            to = chip(i)
            for core in range(2):
                k = 2 * to + core - c * nz
                wanted = (k >= 0) & (k < nz)
                own = (to == z) & (c == core)

                @pl.when(wanted & own)
                def _():
                    pltpu.make_async_copy(source(k), target.at[z], p1_recv.at[at]).start()

                @pl.when(wanted & jnp.logical_not(own))
                def _():
                    pltpu.make_async_remote_copy(
                        source(k), target.at[z], p1_send.at[at], p1_recv.at[at],
                        device_id=(x * nz + to, y, core), device_id_type=MESH,
                    ).start()

    def give_back(at, source, target):
        @pl.loop(0, nz)
        def _(i):
            t = chip(i)
            own = paired & (t == z)

            @pl.when(own)
            def _():
                pltpu.make_async_copy(source.at[t], target.at[place], p1_recv.at[at]).start()

            @pl.when(jnp.logical_not(own))
            def _():
                pltpu.make_async_remote_copy(
                    source.at[t], target.at[place], p1_send.at[at], p1_recv.at[at],
                    device_id=(x * nz + t, y, home), device_id_type=MESH,
                ).start()

    def arrived(at, target):
        pltpu.make_async_copy(target, target, p1_recv.at[at]).wait()

    def sent(at, like):
        @pl.when(paired)
        def _():
            part = like.at[pl.ds(0, nz - 1)]
            pltpu.make_async_copy(part, part, p1_send.at[at]).wait()

        @pl.when(jnp.logical_not(paired))
        def _():
            pltpu.make_async_copy(like, like, p1_send.at[at]).wait()

    fetches[0].wait()
    pack(cot_ref, send_c)
    pl.semaphore_wait(
        barrier, nz - paired.astype(jnp.int32) + beside_count + (nx * ny - 1) + ny
    )
    scatter(1, lambda k: send_c.at[k], recv_c)
    fetches[1].wait()
    pack(in_ref, send_i)
    scatter(2, lambda k: send_i.at[k], recv_i)
    fetches[2].wait()
    scatter(0, lambda k: dec_ref, dec_in)
    fetches[3].wait()
    fetches[4].wait()
    fetches[5].wait()

    old = lax.broadcasted_iota(jnp.int32, (states, states), 0)
    new = lax.broadcasted_iota(jnp.int32, (states, states), 1)
    perm = jnp.where((old % ny) * (nx * nz) + old // ny == new, 1.0, 0.0).astype(BF16)

    @pl.loop(0, 9)
    def _(tap):
        at = pl.ds(pl.multiple_of(tap * ln, ln), ln)
        w_src[at] = dot(win_ref[tap], perm, ((1,), (0,))).astype(BF16)
        w_exc[at] = dot(wout_ref[tap], perm, ((0,), (0,))).astype(BF16)
        w_back[tap] = dot(perm, win_ref[tap], ((0,), (1,))).astype(BF16)

    def unpack(recv, pad):
        t32[...] = recv[...].astype(F32).reshape(block, ln)

        @pl.loop(0, rows)
        def _(r):
            for col in range(2):
                pad[1 + col, 1 + r] = t32[
                    pl.ds(col * rows + r, nz, stride=cells)
                ].astype(BF16)

    def halo(which, pad, act):
        for at, (dr, dc) in enumerate(SIDES):
            there = (-dr, -dc)
            from_rows = {-1: pl.ds(1, 1), 0: pl.ds(1, rows), 1: pl.ds(rows, 1)}[dr]
            to_rows = {-1: pl.ds(rows + 1, 1), 0: pl.ds(1, rows), 1: pl.ds(0, 1)}[dr]
            from_cols = {-1: pl.ds(1, 1), 0: pl.ds(1, 2), 1: pl.ds(2, 1)}[dc]
            to_cols = {-1: pl.ds(3, 1), 0: pl.ds(1, 2), 1: pl.ds(0, 1)}[dc]
            copy = pltpu.make_async_remote_copy(
                pad.at[from_cols, from_rows], pad.at[to_cols, to_rows],
                halo_send.at[which, at], halo_recv.at[which, at],
                device_id=beside(dr, dc), device_id_type=MESH,
            )
            if act == "send":
                pl.when(here(dr, dc))(copy.start)
            elif act == "sent":
                pl.when(here(dr, dc))(copy.wait_send)
            else:
                pl.when(here(*there))(copy.wait_recv)

    def lay_out(pad, cols, flip):
        for tap, (di, dj) in enumerate(TAPS):
            a, b = (2 - di, 2 - dj) if flip else (di, dj)
            cols[:, tap * ln : (tap + 1) * ln] = pad[b : b + 2, a : a + rows].reshape(block, ln)

    def carry_copy(send, recv, which, to):
        return pltpu.make_async_remote_copy(
            send, recv.at[x], car_send.at[which, to], car_recv.at[which, x],
            device_id=(to * nz + z, y, c), device_id_type=MESH,
        )

    def carry_from(recv, which, source):
        return pltpu.make_async_copy(recv.at[source], recv.at[source], car_recv.at[which, source])

    def fold(recv, which, order, needed):
        entry[...] = jnp.zeros_like(entry)
        for source in order:
            @pl.when(needed(source))
            def _():
                carry_from(recv, which, source).wait()
                for h in range(2):
                    entry[h] = (
                        recv[source, h, :cells] + recv[source, h, cells : cells + 1] * entry[h]
                    )

    frame = lambda t: pl.ds(t, cells, stride=nz)

    arrived(1, recv_c)
    unpack(recv_c, pad_c)
    halo(0, pad_c, "send")
    arrived(2, recv_i)
    unpack(recv_i, pad_i)
    halo(1, pad_i, "send")
    arrived(0, dec_in)
    rates = exact_dot(dec_in[...].reshape(nz, states), perm, ((1,), (0,)))
    decp[0] = rates[:, :ln]
    decp[1] = rates[:, ln:]
    halo(0, pad_c, "arrive")
    lay_out(pad_c, cols_c, True)
    value = dot(cols_c[...], w_exc[...], ((1,), (0,)))
    exc[0] = value[:, :ln]
    exc[1] = value[:, ln:]

    for h in range(2):
        def adjoint_step(i, held):
            b, factor = held
            t = nz - 1 - i
            rate = decp[h, pl.ds(t, 1)]
            return rate * (exc[h, frame(t)] + b), factor * rate

        b, factor = lax.fori_loop(
            0, nz, adjoint_step, (jnp.zeros((cells, ln), F32), jnp.ones((1, ln), F32))
        )
        carry_a[h, :cells] = b
        carry_a[h, cells:] = jnp.broadcast_to(factor, (8, ln))
    for to in range(nx):
        pl.when(to < x)(carry_copy(carry_a, carries_a, 0, to).start)

    halo(1, pad_i, "arrive")
    lay_out(pad_i, cols_i, False)
    value = dot(cols_i[...], w_src[...], ((1,), (0,)))
    src[0] = value[:, :ln]
    src[1] = value[:, ln:]
    for h in range(2):
        def state_step(t, level):
            return decp[h, pl.ds(t, 1)] * level + src[h, frame(t)]

        carry_s[h, :cells] = lax.fori_loop(0, nz, state_step, jnp.zeros((cells, ln), F32))
        carry_s[h, cells:] = carry_a[h, cells:]
    for to in range(nx):
        pl.when(to > x)(carry_copy(carry_s, carries_s, 1, to).start)

    fold(carries_a, 0, range(nx - 1, -1, -1), lambda source: source > x)
    for h in range(2):
        def adjoint_final(i, b):
            t = nz - 1 - i
            level = exc[h, frame(t)] + b
            exc[h, frame(t)] = level
            return decp[h, pl.ds(t, 1)] * level

        lax.fori_loop(0, nz, adjoint_final, entry[h])
    adjoint_b = jnp.concatenate([exc[0], exc[1]], axis=1).astype(BF16)
    pad_a[1:3, 1 : 1 + rows] = adjoint_b.reshape(2, rows, nz, states)
    halo(2, pad_a, "send")

    half = ny // 2

    def core_copy(h):
        part = pl.ds(h * half, half)
        return pltpu.make_async_remote_copy(
            grad_b.at[part], from_core.at[part], core_send.at[h], core_recv.at[h],
            device_id=(tm, y, 1 - c), device_id_type=MESH,
        )

    def xy_copy(i):
        to_x, to_y = flat_to(i)
        return pltpu.make_async_remote_copy(
            part_b.at[to_y, to_x], from_xy.at[i], xy_send.at[i], xy_recv.at[i],
            device_id=flat_id(i), device_id_type=MESH,
        )

    def gradient(which, h, levels, cols):
        part = slice(h * half, (h + 1) * half)
        value = dot(levels[h].astype(BF16), cols[...], ((0,), (0,)))
        grad[which, part] = value.reshape(half, nx, nz, 9 * ln)

        @pl.when(c != which)
        def _():
            grad_b[part] = grad[which, part].astype(BF16)
            core_copy(h).start()

    def begin():
        for h in range(2):
            core_copy(h).wait_recv()
            part = slice(h * half, (h + 1) * half)
            part_b[part] = (grad[c, part] + from_core[part].astype(F32)).astype(BF16)

            @pl.loop(0, others)
            def _(i):
                pl.when(flat_to(i)[1] // half == h)(lambda: xy_copy(i).start())

    for h in range(2):
        gradient(0, h, exc, cols_i)
    pl.when(c == 0)(begin)

    fold(carries_s, 1, range(nx), lambda source: source < x)
    for h in range(2):
        def state_final(t, level):
            now = decp[h, pl.ds(t, 1)] * level + src[h, frame(t)]
            src[h, frame(t)] = now
            dg_part[h, pl.ds(t, 1)] = jnp.sum(exc[h, frame(t)] * level, axis=0, keepdims=True)
            return now

        lax.fori_loop(0, nz, state_final, entry[h])
        gradient(1, h, src, cols_c)
    pl.when(c == 1)(begin)

    halo(2, pad_a, "arrive")
    total = skip_ref[...] * pad_c[1:3, 1 : 1 + rows].reshape(block, ln).astype(F32)
    for tap, (di, dj) in enumerate(TAPS):
        a, b = 2 - di, 2 - dj
        total += dot(pad_a[b : b + 2, a : a + rows].reshape(block, states), w_back[tap], ((1,), (0,)))
    t32[...] = total

    @pl.loop(0, nz)
    def _(t):
        send_d[t] = t32[frame(t)].astype(BF16)

    give_back(3, send_d, recv_d)

    dg_old = exact_dot(
        jnp.concatenate([dg_part[0], dg_part[1]], axis=1), perm, ((1,), (1,))
    )
    high = dg_old.astype(BF16).astype(F32)
    mid = (dg_old - high).astype(BF16).astype(F32)
    low = dg_old - high - mid
    mail32[:, 15] = jnp.zeros((nz, ln), F32)
    for at, part in enumerate((high, mid, low)):
        mail32[:, 9 + 2 * at] = part[:, :ln]
        mail32[:, 10 + 2 * at] = part[:, ln:]

    def xy_sum(i, total):
        xy_copy(i).wait_recv()
        return total + from_xy[i].astype(F32)

    summed = lax.fori_loop(0, others, xy_sum, grad[c, y, x] + from_core[y, x].astype(F32))
    for tap in range(9):
        mail32[:, tap] = summed[:, tap * ln : (tap + 1) * ln]
    mail[...] = mail32[...].astype(BF16)

    give_back(4, mail, from_z)

    arrived(3, recv_d)
    t32[...] = recv_d[...].astype(F32).reshape(block, ln)

    @pl.loop(0, rows)
    def _(r):
        dinp_ref[r] = t32[pl.ds(r, wide, stride=rows)].astype(BF16)

    put_dinp = pltpu.make_async_copy(dinp_ref, dinp_hbm, put_sem.at[0])
    put_dinp.start()

    arrived(4, from_z)
    both = [jnp.zeros((16, ln), F32), jnp.zeros((16, ln), F32)]
    for k in range(nz):
        both[k % 2] = both[k % 2] + from_z[k].astype(F32)
    share[:9] = both[0][:9]
    share[9:18] = both[1][:9]
    rest = both[0] + both[1]
    share[18:20] = rest[9:11] + (rest[11:13] + rest[13:15])

    def share_copy(o):
        return pltpu.make_async_remote_copy(
            share, shares.at[spot], ag_send.at[o - 1], ag_recv.at[o - 1],
            device_id=spot_id(o), device_id_type=MESH,
        )

    for o in sorted(range(1, 2 * ny), key=lambda o: -min(o, 2 * ny - o)):
        share_copy(o).start()
    own = pltpu.make_async_copy(share, shares.at[spot], put_sem.at[1])
    own.start()
    for o in range(1, 2 * ny):
        share_copy(o).wait_recv()
    own.wait()
    put_dinp.wait()

    sent(0, dec_in)
    sent(1, send_c)
    sent(2, send_i)
    sent(3, send_d)
    sent(4, mail)
    for which, pad in enumerate((pad_c, pad_i, pad_a)):
        halo(which, pad, "sent")
    for to in range(nx):
        pl.when(to < x)(carry_copy(carry_a, carries_a, 0, to).wait_send)
        pl.when(to > x)(carry_copy(carry_s, carries_s, 1, to).wait_send)
    for h in range(2):
        core_copy(h).wait_send()

    @pl.loop(0, others)
    def _(i):
        xy_copy(i).wait_send()

    for o in range(1, 2 * ny):
        share_copy(o).wait_send()


def finish(ny, ln, wscale, dscale, dinp_hbm, shares_hbm, out_hbm, din_ref, dout_ref, dg_ref, shares, tile, sem):
    fetch = pltpu.make_async_copy(shares_hbm, shares, sem.at[0])
    come = pltpu.make_async_copy(dinp_hbm, tile, sem.at[1])
    go = pltpu.make_async_copy(tile, out_hbm, sem.at[2])
    come.start()
    fetch.start()
    come.wait()
    go.start()
    fetch.wait()
    for j in range(ny):
        both = shares[2 * j] + shares[2 * j + 1]
        din_ref[:, j] = both[:9] * wscale
        dout_ref[:, j] = both[9:18] * wscale
    total = shares[0, 18:20]
    for s in range(1, 2 * ny):
        total += shares[s, 18:20]
    dg_ref[:, :ln] = total[:1] * dscale
    dg_ref[:, ln:] = total[1:] * dscale
    go.wait()


def body(nx, inputs, cotangent, w_in, w_out, decay, skip):
    _, rows, wide, ln = inputs.shape
    ny = lax.axis_size("row")
    nz = lax.axis_size("tm") // nx
    states = w_in.shape[3]
    cells = 2 * rows
    block = cells * nz
    wscale = 1.0 / math.sqrt(nx * nz * ny * rows * wide * 2)
    dscale = 1.0 / math.sqrt(ny * rows * wide * 2)
    vmem = pltpu.VMEM
    dma = pltpu.SemaphoreType.DMA
    scratch = [
        vmem((rows, wide, ln), BF16),
        vmem((rows, wide, ln), BF16),
        vmem((9, ln, states), BF16),
        vmem((9, states, ln), BF16),
        vmem((1, states), F32),
        vmem((1, ln), F32),
        dma((6,)),
        vmem((block, ln), F32),
        vmem((nz, cells, ln), BF16),
        vmem((nz, cells, ln), BF16),
        vmem((nz, cells, ln), BF16),
        vmem((nz, cells, ln), BF16),
        vmem((nz, cells, ln), BF16),
        vmem((nz, cells, ln), BF16),
        vmem((nz, 1, states), F32),
        vmem((2, nz, ln), F32),
        vmem((4, rows + 2, nz, ln), BF16),
        vmem((4, rows + 2, nz, ln), BF16),
        vmem((4, rows + 2, nz, states), BF16),
        vmem((block, 9 * ln), BF16),
        vmem((block, 9 * ln), BF16),
        vmem((9 * ln, states), BF16),
        vmem((9 * ln, states), BF16),
        vmem((9, states, ln), BF16),
        vmem((2, block, ln), F32),
        vmem((2, block, ln), F32),
        vmem((2, cells + 8, ln), F32),
        vmem((nx, 2, cells + 8, ln), F32),
        vmem((2, cells + 8, ln), F32),
        vmem((nx, 2, cells + 8, ln), F32),
        vmem((2, cells, ln), F32),
        vmem((2, nz, ln), F32),
        vmem((2, ny, nx, nz, 9 * ln), F32),
        vmem((ny, nx, nz, 9 * ln), BF16),
        vmem((ny, nx, nz, 9 * ln), BF16),
        vmem((ny, nx, nz, 9 * ln), BF16),
        vmem((nx * ny - 1, nz, 9 * ln), BF16),
        vmem((nz, 16, ln), F32),
        vmem((nz, 16, ln), BF16),
        vmem((nz, 16, ln), BF16),
        vmem((20, ln), F32),
        vmem((rows, wide, ln), BF16),
        dma((2,)),
        dma((5,)),
        dma((5,)),
        dma((3, 8)),
        dma((3, 8)),
        dma((2, nx)),
        dma((2, nx)),
        dma((2,)),
        dma((2,)),
        dma((nx * ny - 1,)),
        dma((nx * ny - 1,)),
        dma((2 * ny - 1,)),
        dma((2 * ny - 1,)),
    ]
    tile = jax.ShapeDtypeStruct((rows, wide, ln), BF16)
    d_inputs, shares = pl.pallas_call(
        functools.partial(kernel, nx, nz, ny, rows, ln),
        out_shape=(tile, jax.ShapeDtypeStruct((2 * ny, 20, ln), F32)),
        in_specs=[pl.BlockSpec(memory_space=pltpu.HBM)] * 6,
        out_specs=(pl.BlockSpec(memory_space=pltpu.HBM), pl.BlockSpec(memory_space=pltpu.HBM)),
        scratch_shapes=scratch,
        compiler_params=pltpu.CompilerParams(
            collective_id=0, has_side_effects=True, vmem_limit_bytes=63 * 1024 * 1024
        ),
        cost_estimate=pl.CostEstimate(
            flops=5 * 2 * block * 9 * ln * states, bytes_accessed=4 * 1024 * 1024, transcendentals=0
        ),
    )(
        inputs.reshape(rows, wide, ln),
        cotangent.reshape(rows, wide, ln),
        w_in.reshape(9, ln, states),
        w_out.reshape(9, states, ln),
        decay,
        skip.reshape(1, ln),
    )
    whole = pl.BlockSpec(memory_space=pltpu.VMEM)
    d_inputs, d_in, d_out, d_decay = pl.pallas_call(
        functools.partial(finish, ny, ln, wscale, dscale),
        out_shape=(
            tile,
            jax.ShapeDtypeStruct((9, ny, ln), F32),
            jax.ShapeDtypeStruct((9, ny, ln), F32),
            jax.ShapeDtypeStruct((1, states), F32),
        ),
        in_specs=[pl.BlockSpec(memory_space=pltpu.HBM)] * 2,
        out_specs=(pl.BlockSpec(memory_space=pltpu.HBM), whole, whole, whole),
        scratch_shapes=[vmem((2 * ny, 20, ln), F32), vmem((rows, wide, ln), BF16), dma((3,))],
        compiler_params=pltpu.CompilerParams(vmem_limit_bytes=63 * 1024 * 1024),
    )(d_inputs, shares)

    def by_channel(grad):
        return jnp.transpose(grad.reshape(3, 3, ny, ln), (2, 0, 1, 3))

    return (d_inputs[None], by_channel(d_in), by_channel(d_out), d_decay)


def solution(mesh, nx=X_CHIPS):
    in_specs = (
        P("tm", "row", "col", None),
        P("tm", "row", "col", None),
        P(),
        P(),
        P("tm", None),
        P(),
    )
    out_specs = (
        P("tm", "row", "col", None),
        P("tm", None, None, None),
        P("tm", None, None, None),
        P("tm", None),
    )
    return jax.shard_map(
        functools.partial(body, nx), mesh=mesh, in_specs=in_specs, out_specs=out_specs,
        check_vma=False,
    )
```

```python
import functools
import math

import jax
import jax.numpy as jnp
from jax import lax
from jax.experimental import pallas as pl
from jax.experimental.pallas import tpu as pltpu
from jax.sharding import PartitionSpec as P

MESH = pl.DeviceIdType.MESH
F32 = jnp.float32
BF16 = jnp.bfloat16
X_CHIPS = 4
TAPS = [(di, dj) for di in range(3) for dj in range(3)]
SIDES = [(0, -1), (0, 1), (-1, -1), (1, 1), (-1, 1), (1, -1), (-1, 0), (1, 0)]


def far(i, n):
    odd = i % 2
    return n // 2 + (1 - odd) * (i // 2) - odd * ((i + 1) // 2)


def dot(a, b, dims):
    return lax.dot_general(a, b, (dims, ((), ())), preferred_element_type=F32)


def exact_dot(a, b, dims):
    high = a.astype(BF16)
    rest = a - high.astype(F32)
    mid = rest.astype(BF16)
    low = (rest - mid.astype(F32)).astype(BF16)
    return dot(high, b, dims) + dot(mid, b, dims) + dot(low, b, dims)


def kernel(
    nx, nz, ny, rows, ln,
    in_hbm, cot_hbm, win_hbm, wout_hbm, dec_hbm, skip_hbm,
    dinp_hbm, shares,
    in_ref, cot_ref, win_ref, wout_ref, dec_ref, skip_ref, fetch_sem,
    t32, send_c, send_i, send_d, recv_c, recv_i, recv_d, dec_in, decp,
    pad_c, pad_i, pad_a, cols_c, cols_i, w_src, w_exc, w_back,
    exc, src,
    carry_a, carries_a, carry_s, carries_s, entry, dg_part,
    grad, grad_b, from_core, part_b, from_xy,
    mail32, mail, from_z, share, dinp_ref, put_sem,
    p1_send, p1_recv, halo_send, halo_recv, car_send, car_recv,
    core_send, core_recv, xy_send, xy_recv, ag_send, ag_recv,
):
    cells = 2 * rows
    wide = 2 * nz
    states = 2 * ln
    block = cells * nz
    tm = lax.axis_index("tm")
    y = lax.axis_index("row")
    c = lax.axis_index("col")
    x = tm // nz
    z = tm % nz
    q = 2 * z + c
    home = q // nz
    place = q % nz
    paired = home == c
    spot = 2 * y + c

    def here(dr, dc):
        return (y + dr >= 0) & (y + dr < ny) & (q + dc >= 0) & (q + dc < wide)

    def beside(dr, dc):
        to = q + dc
        return (x * nz + to // 2, y + dr, to % 2)

    def flat_to(i):
        return (x + far(i // ny, nx)) % nx, (y + far(i % ny, ny)) % ny

    def flat_id(i):
        to_x, to_y = flat_to(i)
        return (to_x * nz + z, to_y, c)

    def spot_id(o):
        to = (spot + o) % (2 * ny)
        return (tm, to // 2, to % 2)

    def chip(i):
        return (z + far(i, nz)) % nz

    fetches = [
        pltpu.make_async_copy(source, target, fetch_sem.at[at])
        for at, (source, target) in enumerate([
            (cot_hbm, cot_ref), (in_hbm, in_ref), (dec_hbm, dec_ref),
            (wout_hbm, wout_ref), (win_hbm, win_ref), (skip_hbm, skip_ref),
        ])
    ]
    for fetch in fetches:
        fetch.start()

    barrier = pltpu.get_barrier_semaphore()

    def greet(device):
        pl.semaphore_signal(barrier, inc=1, device_id=device, device_id_type=MESH)

    @pl.loop(0, nz)
    def _(i):
        t = chip(i)

        @pl.when(jnp.logical_not(paired & (t == z)))
        def _():
            greet((x * nz + t, y, home))

    others = nx * ny - 1

    @pl.loop(0, others)
    def _(i):
        greet(flat_id(i))

    for o in range(1, 2 * ny, 2):
        greet((tm, (y + o // 2) % ny, 1 - c))

    pad_c[...] = jnp.zeros_like(pad_c)
    pad_i[...] = jnp.zeros_like(pad_i)
    pad_a[...] = jnp.zeros_like(pad_a)

    beside_count = jnp.int32(0)
    for dr, dc in SIDES:
        beside_count += here(dr, dc).astype(jnp.int32)

        @pl.when(here(dr, dc))
        def _():
            greet(beside(dr, dc))


    def pack(ref, out):
        t32[...] = ref[...].astype(F32).reshape(block, ln)

        @pl.loop(0, nz)
        def _(k):
            for col in range(2):
                out[k, col * rows : (col + 1) * rows] = t32[
                    pl.ds(2 * k + col, rows, stride=wide)
                ].astype(BF16)

    def scatter(at, source, target):
        @pl.loop(0, nz)
        def _(i):
            to = chip(i)
            for core in range(2):
                k = 2 * to + core - c * nz
                wanted = (k >= 0) & (k < nz)
                own = (to == z) & (c == core)

                @pl.when(wanted & own)
                def _():
                    pltpu.make_async_copy(source(k), target.at[z], p1_recv.at[at]).start()

                @pl.when(wanted & jnp.logical_not(own))
                def _():
                    pltpu.make_async_remote_copy(
                        source(k), target.at[z], p1_send.at[at], p1_recv.at[at],
                        device_id=(x * nz + to, y, core), device_id_type=MESH,
                    ).start()

    def give_back(at, source, target):
        @pl.loop(0, nz)
        def _(i):
            t = chip(i)
            own = paired & (t == z)

            @pl.when(own)
            def _():
                pltpu.make_async_copy(source.at[t], target.at[place], p1_recv.at[at]).start()

            @pl.when(jnp.logical_not(own))
            def _():
                pltpu.make_async_remote_copy(
                    source.at[t], target.at[place], p1_send.at[at], p1_recv.at[at],
                    device_id=(x * nz + t, y, home), device_id_type=MESH,
                ).start()

    def arrived(at, target):
        pltpu.make_async_copy(target, target, p1_recv.at[at]).wait()

    def sent(at, like):
        @pl.when(paired)
        def _():
            part = like.at[pl.ds(0, nz - 1)]
            pltpu.make_async_copy(part, part, p1_send.at[at]).wait()

        @pl.when(jnp.logical_not(paired))
        def _():
            pltpu.make_async_copy(like, like, p1_send.at[at]).wait()

    fetches[0].wait()
    pack(cot_ref, send_c)
    pl.semaphore_wait(
        barrier, nz - paired.astype(jnp.int32) + beside_count + (nx * ny - 1) + ny
    )
    scatter(1, lambda k: send_c.at[k], recv_c)
    fetches[1].wait()
    pack(in_ref, send_i)
    scatter(2, lambda k: send_i.at[k], recv_i)
    fetches[2].wait()
    scatter(0, lambda k: dec_ref, dec_in)
    fetches[3].wait()
    fetches[4].wait()
    fetches[5].wait()

    old = lax.broadcasted_iota(jnp.int32, (states, states), 0)
    new = lax.broadcasted_iota(jnp.int32, (states, states), 1)
    perm = jnp.where((old % ny) * (nx * nz) + old // ny == new, 1.0, 0.0).astype(BF16)

    @pl.loop(0, 9)
    def _(tap):
        at = pl.ds(pl.multiple_of(tap * ln, ln), ln)
        w_src[at] = dot(win_ref[tap], perm, ((1,), (0,))).astype(BF16)
        w_exc[at] = dot(wout_ref[tap], perm, ((0,), (0,))).astype(BF16)
        w_back[tap] = dot(perm, win_ref[tap], ((0,), (1,))).astype(BF16)

    def unpack(recv, pad):
        t32[...] = recv[...].astype(F32).reshape(block, ln)

        @pl.loop(0, rows)
        def _(r):
            for col in range(2):
                pad[1 + col, 1 + r] = t32[
                    pl.ds(col * rows + r, nz, stride=cells)
                ].astype(BF16)

    def halo(which, pad, act):
        for at, (dr, dc) in enumerate(SIDES):
            there = (-dr, -dc)
            from_rows = {-1: pl.ds(1, 1), 0: pl.ds(1, rows), 1: pl.ds(rows, 1)}[dr]
            to_rows = {-1: pl.ds(rows + 1, 1), 0: pl.ds(1, rows), 1: pl.ds(0, 1)}[dr]
            from_cols = {-1: pl.ds(1, 1), 0: pl.ds(1, 2), 1: pl.ds(2, 1)}[dc]
            to_cols = {-1: pl.ds(3, 1), 0: pl.ds(1, 2), 1: pl.ds(0, 1)}[dc]
            copy = pltpu.make_async_remote_copy(
                pad.at[from_cols, from_rows], pad.at[to_cols, to_rows],
                halo_send.at[which, at], halo_recv.at[which, at],
                device_id=beside(dr, dc), device_id_type=MESH,
            )
            if act == "send":
                pl.when(here(dr, dc))(copy.start)
            elif act == "sent":
                pl.when(here(dr, dc))(copy.wait_send)
            else:
                pl.when(here(*there))(copy.wait_recv)

    def lay_out(pad, cols, flip):
        for tap, (di, dj) in enumerate(TAPS):
            a, b = (2 - di, 2 - dj) if flip else (di, dj)
            cols[:, tap * ln : (tap + 1) * ln] = pad[b : b + 2, a : a + rows].reshape(block, ln)

    def carry_copy(send, recv, which, to):
        return pltpu.make_async_remote_copy(
            send, recv.at[x], car_send.at[which, to], car_recv.at[which, x],
            device_id=(to * nz + z, y, c), device_id_type=MESH,
        )

    def carry_from(recv, which, source):
        return pltpu.make_async_copy(recv.at[source], recv.at[source], car_recv.at[which, source])

    def fold(recv, which, order, needed):
        entry[...] = jnp.zeros_like(entry)
        for source in order:
            @pl.when(needed(source))
            def _():
                carry_from(recv, which, source).wait()
                for h in range(2):
                    held = recv[source, h].astype(F32)
                    factor = (
                        held[cells : cells + 1] + held[cells + 1 : cells + 2]
                        + held[cells + 2 : cells + 3]
                    )
                    entry[h] = held[:cells] + factor * entry[h]

    frame = lambda t: pl.ds(t, cells, stride=nz)

    arrived(1, recv_c)
    unpack(recv_c, pad_c)
    halo(0, pad_c, "send")
    arrived(2, recv_i)
    unpack(recv_i, pad_i)
    halo(1, pad_i, "send")
    arrived(0, dec_in)
    rates = exact_dot(dec_in[...].reshape(nz, states), perm, ((1,), (0,)))
    decp[0] = rates[:, :ln]
    decp[1] = rates[:, ln:]
    halo(0, pad_c, "arrive")
    lay_out(pad_c, cols_c, True)
    value = dot(cols_c[...], w_exc[...], ((1,), (0,)))
    exc[0] = value[:, :ln]
    exc[1] = value[:, ln:]

    for h in range(2):
        def adjoint_step(i, held):
            b, factor = held
            t = nz - 1 - i
            rate = decp[h, pl.ds(t, 1)]
            return rate * (exc[h, frame(t)] + b), factor * rate

        b, factor = lax.fori_loop(
            0, nz, adjoint_step, (jnp.zeros((cells, ln), F32), jnp.ones((1, ln), F32))
        )
        high = factor.astype(BF16).astype(F32)
        mid = (factor - high).astype(BF16).astype(F32)
        row = lax.broadcasted_iota(jnp.int32, (16, ln), 0)
        parts = jnp.where(
            row == 0, high, jnp.where(row == 1, mid, jnp.where(row == 2, factor - high - mid, 0.0))
        )
        carry_a[h, :cells] = b.astype(BF16)
        carry_a[h, cells:] = parts.astype(BF16)
    for to in range(nx):
        pl.when(to < x)(carry_copy(carry_a, carries_a, 0, to).start)

    halo(1, pad_i, "arrive")
    lay_out(pad_i, cols_i, False)
    value = dot(cols_i[...], w_src[...], ((1,), (0,)))
    src[0] = value[:, :ln]
    src[1] = value[:, ln:]
    for h in range(2):
        def state_step(t, level):
            return decp[h, pl.ds(t, 1)] * level + src[h, frame(t)]

        carry_s[h, :cells] = lax.fori_loop(
            0, nz, state_step, jnp.zeros((cells, ln), F32)
        ).astype(BF16)
        carry_s[h, cells:] = carry_a[h, cells:]
    for to in range(nx):
        pl.when(to > x)(carry_copy(carry_s, carries_s, 1, to).start)

    fold(carries_a, 0, range(nx - 1, -1, -1), lambda source: source > x)
    for h in range(2):
        def adjoint_final(i, b):
            t = nz - 1 - i
            level = exc[h, frame(t)] + b
            exc[h, frame(t)] = level
            return decp[h, pl.ds(t, 1)] * level

        lax.fori_loop(0, nz, adjoint_final, entry[h])
    adjoint_b = jnp.concatenate([exc[0], exc[1]], axis=1).astype(BF16)
    pad_a[1:3, 1 : 1 + rows] = adjoint_b.reshape(2, rows, nz, states)
    halo(2, pad_a, "send")

    half = ny // 2

    def core_copy(h):
        part = pl.ds(h * half, half)
        return pltpu.make_async_remote_copy(
            grad_b.at[part], from_core.at[part], core_send.at[h], core_recv.at[h],
            device_id=(tm, y, 1 - c), device_id_type=MESH,
        )

    def xy_copy(i):
        to_x, to_y = flat_to(i)
        return pltpu.make_async_remote_copy(
            part_b.at[to_y, to_x], from_xy.at[i], xy_send.at[i], xy_recv.at[i],
            device_id=flat_id(i), device_id_type=MESH,
        )

    def gradient(which, h, levels, cols):
        part = slice(h * half, (h + 1) * half)
        value = dot(levels[h].astype(BF16), cols[...], ((0,), (0,)))
        grad[which, part] = value.reshape(half, nx, nz, 9 * ln)

        @pl.when(c != which)
        def _():
            grad_b[part] = grad[which, part].astype(BF16)
            core_copy(h).start()

    def begin():
        for h in range(2):
            core_copy(h).wait_recv()
            part = slice(h * half, (h + 1) * half)
            part_b[part] = (grad[c, part] + from_core[part].astype(F32)).astype(BF16)

            @pl.loop(0, others)
            def _(i):
                pl.when(flat_to(i)[1] // half == h)(lambda: xy_copy(i).start())

    for h in range(2):
        gradient(0, h, exc, cols_i)
    pl.when(c == 0)(begin)

    fold(carries_s, 1, range(nx), lambda source: source < x)
    for h in range(2):
        def state_final(t, level):
            now = decp[h, pl.ds(t, 1)] * level + src[h, frame(t)]
            src[h, frame(t)] = now
            dg_part[h, pl.ds(t, 1)] = jnp.sum(exc[h, frame(t)] * level, axis=0, keepdims=True)
            return now

        lax.fori_loop(0, nz, state_final, entry[h])
        gradient(1, h, src, cols_c)
    pl.when(c == 1)(begin)

    halo(2, pad_a, "arrive")
    total = skip_ref[...] * pad_c[1:3, 1 : 1 + rows].reshape(block, ln).astype(F32)
    for tap, (di, dj) in enumerate(TAPS):
        a, b = 2 - di, 2 - dj
        total += dot(pad_a[b : b + 2, a : a + rows].reshape(block, states), w_back[tap], ((1,), (0,)))
    t32[...] = total

    @pl.loop(0, nz)
    def _(t):
        send_d[t] = t32[frame(t)].astype(BF16)

    give_back(3, send_d, recv_d)

    dg_old = exact_dot(
        jnp.concatenate([dg_part[0], dg_part[1]], axis=1), perm, ((1,), (1,))
    )
    high = dg_old.astype(BF16).astype(F32)
    mid = (dg_old - high).astype(BF16).astype(F32)
    low = dg_old - high - mid
    mail32[:, 15] = jnp.zeros((nz, ln), F32)
    for at, part in enumerate((high, mid, low)):
        mail32[:, 9 + 2 * at] = part[:, :ln]
        mail32[:, 10 + 2 * at] = part[:, ln:]

    def xy_sum(i, total):
        xy_copy(i).wait_recv()
        return total + from_xy[i].astype(F32)

    summed = lax.fori_loop(0, others, xy_sum, grad[c, y, x] + from_core[y, x].astype(F32))
    for tap in range(9):
        mail32[:, tap] = summed[:, tap * ln : (tap + 1) * ln]
    mail[...] = mail32[...].astype(BF16)

    give_back(4, mail, from_z)

    arrived(3, recv_d)
    t32[...] = recv_d[...].astype(F32).reshape(block, ln)

    @pl.loop(0, rows)
    def _(r):
        dinp_ref[r] = t32[pl.ds(r, wide, stride=rows)].astype(BF16)

    put_dinp = pltpu.make_async_copy(dinp_ref, dinp_hbm, put_sem.at[0])
    put_dinp.start()

    arrived(4, from_z)
    both = [jnp.zeros((16, ln), F32), jnp.zeros((16, ln), F32)]
    for k in range(nz):
        both[k % 2] = both[k % 2] + from_z[k].astype(F32)
    share[:9] = both[0][:9]
    share[9:18] = both[1][:9]
    rest = both[0] + both[1]
    share[18:20] = rest[9:11] + (rest[11:13] + rest[13:15])

    def share_copy(o):
        return pltpu.make_async_remote_copy(
            share, shares.at[spot], ag_send.at[o - 1], ag_recv.at[o - 1],
            device_id=spot_id(o), device_id_type=MESH,
        )

    for o in sorted(range(1, 2 * ny), key=lambda o: -min(o, 2 * ny - o)):
        share_copy(o).start()
    own = pltpu.make_async_copy(share, shares.at[spot], put_sem.at[1])
    own.start()
    sent(0, dec_in)
    sent(1, send_c)
    sent(2, send_i)
    sent(3, send_d)
    sent(4, mail)
    for which, pad in enumerate((pad_c, pad_i, pad_a)):
        halo(which, pad, "sent")
    for to in range(nx):
        pl.when(to < x)(carry_copy(carry_a, carries_a, 0, to).wait_send)
        pl.when(to > x)(carry_copy(carry_s, carries_s, 1, to).wait_send)
    for h in range(2):
        core_copy(h).wait_send()

    @pl.loop(0, others)
    def _(i):
        xy_copy(i).wait_send()

    for o in range(1, 2 * ny):
        share_copy(o).wait_recv()
    own.wait()
    put_dinp.wait()

    for o in range(1, 2 * ny):
        share_copy(o).wait_send()


def finish(ny, ln, wscale, dscale, dinp_hbm, shares_hbm, out_hbm, din_ref, dout_ref, dg_ref, shares, tile, sem):
    fetch = pltpu.make_async_copy(shares_hbm, shares, sem.at[0])
    come = pltpu.make_async_copy(dinp_hbm, tile, sem.at[1])
    go = pltpu.make_async_copy(tile, out_hbm, sem.at[2])
    come.start()
    fetch.start()
    come.wait()
    go.start()
    fetch.wait()
    for j in range(ny):
        both = shares[2 * j] + shares[2 * j + 1]
        din_ref[:, j] = both[:9] * wscale
        dout_ref[:, j] = both[9:18] * wscale
    total = shares[0, 18:20]
    for s in range(1, 2 * ny):
        total += shares[s, 18:20]
    dg_ref[:, :ln] = total[:1] * dscale
    dg_ref[:, ln:] = total[1:] * dscale
    go.wait()


def body(nx, inputs, cotangent, w_in, w_out, decay, skip):
    _, rows, wide, ln = inputs.shape
    ny = lax.axis_size("row")
    nz = lax.axis_size("tm") // nx
    states = w_in.shape[3]
    cells = 2 * rows
    block = cells * nz
    wscale = 1.0 / math.sqrt(nx * nz * ny * rows * wide * 2)
    dscale = 1.0 / math.sqrt(ny * rows * wide * 2)
    vmem = pltpu.VMEM
    dma = pltpu.SemaphoreType.DMA
    scratch = [
        vmem((rows, wide, ln), BF16),
        vmem((rows, wide, ln), BF16),
        vmem((9, ln, states), BF16),
        vmem((9, states, ln), BF16),
        vmem((1, states), F32),
        vmem((1, ln), F32),
        dma((6,)),
        vmem((block, ln), F32),
        vmem((nz, cells, ln), BF16),
        vmem((nz, cells, ln), BF16),
        vmem((nz, cells, ln), BF16),
        vmem((nz, cells, ln), BF16),
        vmem((nz, cells, ln), BF16),
        vmem((nz, cells, ln), BF16),
        vmem((nz, 1, states), F32),
        vmem((2, nz, ln), F32),
        vmem((4, rows + 2, nz, ln), BF16),
        vmem((4, rows + 2, nz, ln), BF16),
        vmem((4, rows + 2, nz, states), BF16),
        vmem((block, 9 * ln), BF16),
        vmem((block, 9 * ln), BF16),
        vmem((9 * ln, states), BF16),
        vmem((9 * ln, states), BF16),
        vmem((9, states, ln), BF16),
        vmem((2, block, ln), F32),
        vmem((2, block, ln), F32),
        vmem((2, cells + 16, ln), BF16),
        vmem((nx, 2, cells + 16, ln), BF16),
        vmem((2, cells + 16, ln), BF16),
        vmem((nx, 2, cells + 16, ln), BF16),
        vmem((2, cells, ln), F32),
        vmem((2, nz, ln), F32),
        vmem((2, ny, nx, nz, 9 * ln), F32),
        vmem((ny, nx, nz, 9 * ln), BF16),
        vmem((ny, nx, nz, 9 * ln), BF16),
        vmem((ny, nx, nz, 9 * ln), BF16),
        vmem((nx * ny - 1, nz, 9 * ln), BF16),
        vmem((nz, 16, ln), F32),
        vmem((nz, 16, ln), BF16),
        vmem((nz, 16, ln), BF16),
        vmem((20, ln), F32),
        vmem((rows, wide, ln), BF16),
        dma((2,)),
        dma((5,)),
        dma((5,)),
        dma((3, 8)),
        dma((3, 8)),
        dma((2, nx)),
        dma((2, nx)),
        dma((2,)),
        dma((2,)),
        dma((nx * ny - 1,)),
        dma((nx * ny - 1,)),
        dma((2 * ny - 1,)),
        dma((2 * ny - 1,)),
    ]
    tile = jax.ShapeDtypeStruct((rows, wide, ln), BF16)
    d_inputs, shares = pl.pallas_call(
        functools.partial(kernel, nx, nz, ny, rows, ln),
        out_shape=(tile, jax.ShapeDtypeStruct((2 * ny, 20, ln), F32)),
        in_specs=[pl.BlockSpec(memory_space=pltpu.HBM)] * 6,
        out_specs=(pl.BlockSpec(memory_space=pltpu.HBM), pl.BlockSpec(memory_space=pltpu.HBM)),
        scratch_shapes=scratch,
        compiler_params=pltpu.CompilerParams(
            collective_id=0, has_side_effects=True, vmem_limit_bytes=63 * 1024 * 1024
        ),
        cost_estimate=pl.CostEstimate(
            flops=5 * 2 * block * 9 * ln * states, bytes_accessed=4 * 1024 * 1024, transcendentals=0
        ),
    )(
        inputs.reshape(rows, wide, ln),
        cotangent.reshape(rows, wide, ln),
        w_in.reshape(9, ln, states),
        w_out.reshape(9, states, ln),
        decay,
        skip.reshape(1, ln),
    )
    whole = pl.BlockSpec(memory_space=pltpu.VMEM)
    d_inputs, d_in, d_out, d_decay = pl.pallas_call(
        functools.partial(finish, ny, ln, wscale, dscale),
        out_shape=(
            tile,
            jax.ShapeDtypeStruct((9, ny, ln), F32),
            jax.ShapeDtypeStruct((9, ny, ln), F32),
            jax.ShapeDtypeStruct((1, states), F32),
        ),
        in_specs=[pl.BlockSpec(memory_space=pltpu.HBM)] * 2,
        out_specs=(pl.BlockSpec(memory_space=pltpu.HBM), whole, whole, whole),
        scratch_shapes=[vmem((2 * ny, 20, ln), F32), vmem((rows, wide, ln), BF16), dma((3,))],
        compiler_params=pltpu.CompilerParams(vmem_limit_bytes=63 * 1024 * 1024),
    )(d_inputs, shares)

    def by_channel(grad):
        return jnp.transpose(grad.reshape(3, 3, ny, ln), (2, 0, 1, 3))

    return (d_inputs[None], by_channel(d_in), by_channel(d_out), d_decay)


def solution(mesh, nx=X_CHIPS):
    in_specs = (
        P("tm", "row", "col", None),
        P("tm", "row", "col", None),
        P(),
        P(),
        P("tm", None),
        P(),
    )
    out_specs = (
        P("tm", "row", "col", None),
        P("tm", None, None, None),
        P("tm", None, None, None),
        P("tm", None),
    )
    return jax.shard_map(
        functools.partial(body, nx), mesh=mesh, in_specs=in_specs, out_specs=out_specs,
        check_vma=False,
    )
```

```python
import functools
import math

import jax
import jax.numpy as jnp
from jax import lax
from jax.experimental import pallas as pl
from jax.experimental.pallas import tpu as pltpu
from jax.sharding import PartitionSpec as P

MESH = pl.DeviceIdType.MESH
F32 = jnp.float32
BF16 = jnp.bfloat16
X_CHIPS = 4
TAPS = [(di, dj) for di in range(3) for dj in range(3)]
SIDES = [(0, -1), (0, 1), (-1, -1), (1, 1), (-1, 1), (1, -1), (-1, 0), (1, 0)]


def far(i, n):
    odd = i % 2
    return n // 2 + (1 - odd) * (i // 2) - odd * ((i + 1) // 2)


def dot(a, b, dims):
    return lax.dot_general(a, b, (dims, ((), ())), preferred_element_type=F32)


def exact_dot(a, b, dims):
    high = a.astype(BF16)
    rest = a - high.astype(F32)
    mid = rest.astype(BF16)
    low = (rest - mid.astype(F32)).astype(BF16)
    return dot(high, b, dims) + dot(mid, b, dims) + dot(low, b, dims)


def kernel(
    nx, nz, ny, rows, ln,
    in_hbm, cot_hbm, win_hbm, wout_hbm, dec_hbm, skip_hbm,
    dinp_hbm, shares,
    in_ref, cot_ref, win_ref, wout_ref, dec_ref, skip_ref, fetch_sem,
    t32, send_c, send_i, send_d, recv_c, recv_i, recv_d, dec_in, decp,
    pad_c, pad_i, pad_a, cols_c, cols_i, w_src, w_exc, w_back,
    exc, src,
    carry_a, carries_a, carry_s, carries_s, entry, dg_part,
    grad, grad_b, from_core, part_b, from_xy,
    mail32, mail, from_z, share, dinp_ref, put_sem,
    p1_send, p1_recv, halo_send, halo_recv, car_send, car_recv,
    core_send, core_recv, xy_send, xy_recv, ag_send, ag_recv,
):
    cells = 2 * rows
    wide = 2 * nz
    states = 2 * ln
    block = cells * nz
    tm = lax.axis_index("tm")
    y = lax.axis_index("row")
    c = lax.axis_index("col")
    x = tm // nz
    z = tm % nz
    q = 2 * z + c
    home = q // nz
    place = q % nz
    paired = home == c
    spot = 2 * y + c

    def here(dr, dc):
        return (y + dr >= 0) & (y + dr < ny) & (q + dc >= 0) & (q + dc < wide)

    def beside(dr, dc):
        to = q + dc
        return (x * nz + to // 2, y + dr, to % 2)

    def flat_to(i):
        return (x + far(i // ny, nx)) % nx, (y + far(i % ny, ny)) % ny

    def flat_id(i):
        to_x, to_y = flat_to(i)
        return (to_x * nz + z, to_y, c)

    def spot_id(o):
        to = (spot + o) % (2 * ny)
        return (tm, to // 2, to % 2)

    def chip(i):
        return (z + far(i, nz)) % nz

    fetches = [
        pltpu.make_async_copy(source, target, fetch_sem.at[at])
        for at, (source, target) in enumerate([
            (cot_hbm, cot_ref), (in_hbm, in_ref), (dec_hbm, dec_ref),
            (wout_hbm, wout_ref), (win_hbm, win_ref), (skip_hbm, skip_ref),
        ])
    ]
    for fetch in fetches:
        fetch.start()

    barrier = pltpu.get_barrier_semaphore()

    def greet(device):
        pl.semaphore_signal(barrier, inc=1, device_id=device, device_id_type=MESH)

    @pl.loop(0, nz)
    def _(i):
        t = chip(i)

        @pl.when(jnp.logical_not(paired & (t == z)))
        def _():
            greet((x * nz + t, y, home))

    others = nx * ny - 1

    @pl.loop(0, others)
    def _(i):
        greet(flat_id(i))

    for o in range(1, 2 * ny, 2):
        greet((tm, (y + o // 2) % ny, 1 - c))

    pad_c[...] = jnp.zeros_like(pad_c)
    pad_i[...] = jnp.zeros_like(pad_i)
    pad_a[...] = jnp.zeros_like(pad_a)

    beside_count = jnp.int32(0)
    for dr, dc in SIDES:
        beside_count += here(dr, dc).astype(jnp.int32)

        @pl.when(here(dr, dc))
        def _():
            greet(beside(dr, dc))


    def pack(ref, out):
        t32[...] = ref[...].astype(F32).reshape(block, ln)

        @pl.loop(0, nz)
        def _(k):
            for col in range(2):
                out[k, col * rows : (col + 1) * rows] = t32[
                    pl.ds(2 * k + col, rows, stride=wide)
                ].astype(BF16)

    def scatter(at, source, target):
        @pl.loop(0, nz)
        def _(i):
            to = chip(i)
            for core in range(2):
                k = 2 * to + core - c * nz
                wanted = (k >= 0) & (k < nz)
                own = (to == z) & (c == core)

                @pl.when(wanted & own)
                def _():
                    pltpu.make_async_copy(source(k), target.at[z], p1_recv.at[at]).start()

                @pl.when(wanted & jnp.logical_not(own))
                def _():
                    pltpu.make_async_remote_copy(
                        source(k), target.at[z], p1_send.at[at], p1_recv.at[at],
                        device_id=(x * nz + to, y, core), device_id_type=MESH,
                    ).start()

    def give_back(at, source, target):
        @pl.loop(0, nz)
        def _(i):
            t = chip(i)
            own = paired & (t == z)

            @pl.when(own)
            def _():
                pltpu.make_async_copy(source.at[t], target.at[place], p1_recv.at[at]).start()

            @pl.when(jnp.logical_not(own))
            def _():
                pltpu.make_async_remote_copy(
                    source.at[t], target.at[place], p1_send.at[at], p1_recv.at[at],
                    device_id=(x * nz + t, y, home), device_id_type=MESH,
                ).start()

    def arrived(at, target):
        pltpu.make_async_copy(target, target, p1_recv.at[at]).wait()

    def sent(at, like):
        @pl.when(paired)
        def _():
            part = like.at[pl.ds(0, nz - 1)]
            pltpu.make_async_copy(part, part, p1_send.at[at]).wait()

        @pl.when(jnp.logical_not(paired))
        def _():
            pltpu.make_async_copy(like, like, p1_send.at[at]).wait()

    fetches[0].wait()
    pack(cot_ref, send_c)
    pl.semaphore_wait(
        barrier, nz - paired.astype(jnp.int32) + beside_count + (nx * ny - 1) + ny
    )
    scatter(1, lambda k: send_c.at[k], recv_c)
    fetches[1].wait()
    pack(in_ref, send_i)
    scatter(2, lambda k: send_i.at[k], recv_i)
    fetches[2].wait()
    scatter(0, lambda k: dec_ref, dec_in)
    fetches[3].wait()
    fetches[4].wait()
    fetches[5].wait()

    old = lax.broadcasted_iota(jnp.int32, (states, states), 0)
    new = lax.broadcasted_iota(jnp.int32, (states, states), 1)
    perm = jnp.where((old % ny) * (nx * nz) + old // ny == new, 1.0, 0.0).astype(BF16)

    @pl.loop(0, 9)
    def _(tap):
        at = pl.ds(pl.multiple_of(tap * ln, ln), ln)
        w_src[at] = dot(win_ref[tap], perm, ((1,), (0,))).astype(BF16)
        w_exc[at] = dot(wout_ref[tap], perm, ((0,), (0,))).astype(BF16)
        w_back[tap] = dot(perm, win_ref[tap], ((0,), (1,))).astype(BF16)

    def unpack(recv, pad):
        t32[...] = recv[...].astype(F32).reshape(block, ln)

        @pl.loop(0, rows)
        def _(r):
            for col in range(2):
                pad[1 + col, 1 + r] = t32[
                    pl.ds(col * rows + r, nz, stride=cells)
                ].astype(BF16)

    def halo(which, pad, act):
        for at, (dr, dc) in enumerate(SIDES):
            there = (-dr, -dc)
            from_rows = {-1: pl.ds(1, 1), 0: pl.ds(1, rows), 1: pl.ds(rows, 1)}[dr]
            to_rows = {-1: pl.ds(rows + 1, 1), 0: pl.ds(1, rows), 1: pl.ds(0, 1)}[dr]
            from_cols = {-1: pl.ds(1, 1), 0: pl.ds(1, 2), 1: pl.ds(2, 1)}[dc]
            to_cols = {-1: pl.ds(3, 1), 0: pl.ds(1, 2), 1: pl.ds(0, 1)}[dc]
            copy = pltpu.make_async_remote_copy(
                pad.at[from_cols, from_rows], pad.at[to_cols, to_rows],
                halo_send.at[which, at], halo_recv.at[which, at],
                device_id=beside(dr, dc), device_id_type=MESH,
            )
            if act == "send":
                pl.when(here(dr, dc))(copy.start)
            elif act == "sent":
                pl.when(here(dr, dc))(copy.wait_send)
            else:
                pl.when(here(*there))(copy.wait_recv)

    def lay_out(pad, cols, flip):
        for tap, (di, dj) in enumerate(TAPS):
            a, b = (2 - di, 2 - dj) if flip else (di, dj)
            cols[:, tap * ln : (tap + 1) * ln] = pad[b : b + 2, a : a + rows].reshape(block, ln)

    def carry_copy(send, recv, which, to):
        return pltpu.make_async_remote_copy(
            send, recv.at[x], car_send.at[which, to], car_recv.at[which, x],
            device_id=(to * nz + z, y, c), device_id_type=MESH,
        )

    def carry_from(recv, which, source):
        return pltpu.make_async_copy(recv.at[source], recv.at[source], car_recv.at[which, source])

    def fold(recv, which, order, needed):
        entry[...] = jnp.zeros_like(entry)
        for source in order:
            @pl.when(needed(source))
            def _():
                carry_from(recv, which, source).wait()
                for h in range(2):
                    held = recv[source, h].astype(F32)
                    factor = (
                        held[cells : cells + 1] + held[cells + 1 : cells + 2]
                        + held[cells + 2 : cells + 3]
                    )
                    entry[h] = held[:cells] + factor * entry[h]

    frame = lambda t: pl.ds(t, cells, stride=nz)

    arrived(1, recv_c)
    unpack(recv_c, pad_c)
    halo(0, pad_c, "send")
    arrived(2, recv_i)
    unpack(recv_i, pad_i)
    halo(1, pad_i, "send")
    arrived(0, dec_in)
    rates = exact_dot(dec_in[...].reshape(nz, states), perm, ((1,), (0,)))
    decp[0] = rates[:, :ln]
    decp[1] = rates[:, ln:]
    halo(0, pad_c, "arrive")
    lay_out(pad_c, cols_c, True)
    value = dot(cols_c[...], w_exc[...], ((1,), (0,)))
    exc[0] = value[:, :ln]
    exc[1] = value[:, ln:]

    for h in range(2):
        def adjoint_step(i, held):
            b, factor = held
            t = nz - 1 - i
            rate = decp[h, pl.ds(t, 1)]
            return rate * (exc[h, frame(t)] + b), factor * rate

        b, factor = lax.fori_loop(
            0, nz, adjoint_step, (jnp.zeros((cells, ln), F32), jnp.ones((1, ln), F32))
        )
        high = factor.astype(BF16).astype(F32)
        mid = (factor - high).astype(BF16).astype(F32)
        row = lax.broadcasted_iota(jnp.int32, (16, ln), 0)
        parts = jnp.where(
            row == 0, high, jnp.where(row == 1, mid, jnp.where(row == 2, factor - high - mid, 0.0))
        )
        carry_a[h, :cells] = b.astype(BF16)
        carry_a[h, cells:] = parts.astype(BF16)
    for to in range(nx):
        pl.when(to < x)(carry_copy(carry_a, carries_a, 0, to).start)

    halo(1, pad_i, "arrive")
    lay_out(pad_i, cols_i, False)
    value = dot(cols_i[...], w_src[...], ((1,), (0,)))
    src[0] = value[:, :ln]
    src[1] = value[:, ln:]
    for h in range(2):
        def state_step(t, level):
            return decp[h, pl.ds(t, 1)] * level + src[h, frame(t)]

        carry_s[h, :cells] = lax.fori_loop(
            0, nz, state_step, jnp.zeros((cells, ln), F32)
        ).astype(BF16)
        carry_s[h, cells:] = carry_a[h, cells:]
    for to in range(nx):
        pl.when(to > x)(carry_copy(carry_s, carries_s, 1, to).start)

    fold(carries_a, 0, range(nx - 1, -1, -1), lambda source: source > x)
    for h in range(2):
        def adjoint_final(i, b):
            t = nz - 1 - i
            level = exc[h, frame(t)] + b
            exc[h, frame(t)] = level
            return decp[h, pl.ds(t, 1)] * level

        lax.fori_loop(0, nz, adjoint_final, entry[h])
    adjoint_b = jnp.concatenate([exc[0], exc[1]], axis=1).astype(BF16)
    pad_a[1:3, 1 : 1 + rows] = adjoint_b.reshape(2, rows, nz, states)
    halo(2, pad_a, "send")

    half = ny // 2

    def core_copy(h):
        part = pl.ds(h * half, half)
        return pltpu.make_async_remote_copy(
            grad_b.at[part], from_core.at[part], core_send.at[h], core_recv.at[h],
            device_id=(tm, y, 1 - c), device_id_type=MESH,
        )

    def xy_copy(i):
        to_x, to_y = flat_to(i)
        return pltpu.make_async_remote_copy(
            part_b.at[to_y, to_x], from_xy.at[i], xy_send.at[i], xy_recv.at[i],
            device_id=flat_id(i), device_id_type=MESH,
        )

    def gradient(which, h, levels, cols):
        part = slice(h * half, (h + 1) * half)
        value = dot(levels[h].astype(BF16), cols[...], ((0,), (0,)))
        grad[which, part] = value.reshape(half, nx, nz, 9 * ln)

        @pl.when(c != which)
        def _():
            grad_b[part] = grad[which, part].astype(BF16)
            core_copy(h).start()

    def begin():
        for h in range(2):
            core_copy(h).wait_recv()
            part = slice(h * half, (h + 1) * half)
            part_b[part] = (grad[c, part] + from_core[part].astype(F32)).astype(BF16)

            @pl.loop(0, others)
            def _(i):
                pl.when(flat_to(i)[1] // half == h)(lambda: xy_copy(i).start())

    for h in range(2):
        gradient(0, h, exc, cols_i)
    pl.when(c == 0)(begin)

    fold(carries_s, 1, range(nx), lambda source: source < x)
    for h in range(2):
        def state_final(t, level):
            now = decp[h, pl.ds(t, 1)] * level + src[h, frame(t)]
            src[h, frame(t)] = now
            dg_part[h, pl.ds(t, 1)] = jnp.sum(exc[h, frame(t)] * level, axis=0, keepdims=True)
            return now

        lax.fori_loop(0, nz, state_final, entry[h])
        gradient(1, h, src, cols_c)
    pl.when(c == 1)(begin)

    halo(2, pad_a, "arrive")
    total = skip_ref[...] * pad_c[1:3, 1 : 1 + rows].reshape(block, ln).astype(F32)
    for tap, (di, dj) in enumerate(TAPS):
        a, b = 2 - di, 2 - dj
        total += dot(pad_a[b : b + 2, a : a + rows].reshape(block, states), w_back[tap], ((1,), (0,)))
    t32[...] = total

    @pl.loop(0, nz)
    def _(t):
        send_d[t] = t32[frame(t)].astype(BF16)

    give_back(3, send_d, recv_d)

    dg_old = exact_dot(
        jnp.concatenate([dg_part[0], dg_part[1]], axis=1), perm, ((1,), (1,))
    )
    high = dg_old.astype(BF16).astype(F32)
    mid = (dg_old - high).astype(BF16).astype(F32)
    low = dg_old - high - mid
    mail32[:, 15] = jnp.zeros((nz, ln), F32)
    for at, part in enumerate((high, mid, low)):
        mail32[:, 9 + 2 * at] = part[:, :ln]
        mail32[:, 10 + 2 * at] = part[:, ln:]

    def xy_sum(i, total):
        xy_copy(i).wait_recv()
        return total + from_xy[i].astype(F32)

    summed = lax.fori_loop(0, others, xy_sum, grad[c, y, x] + from_core[y, x].astype(F32))
    for tap in range(9):
        mail32[:, tap] = summed[:, tap * ln : (tap + 1) * ln]
    mail[...] = mail32[...].astype(BF16)

    give_back(4, mail, from_z)

    arrived(3, recv_d)
    t32[...] = recv_d[...].astype(F32).reshape(block, ln)

    @pl.loop(0, rows)
    def _(r):
        dinp_ref[r] = t32[pl.ds(r, wide, stride=rows)].astype(BF16)

    put_dinp = pltpu.make_async_copy(dinp_ref, dinp_hbm, put_sem.at[0])
    put_dinp.start()

    arrived(4, from_z)
    both = [jnp.zeros((16, ln), F32), jnp.zeros((16, ln), F32)]
    for k in range(nz):
        both[k % 2] = both[k % 2] + from_z[k].astype(F32)
    share[:9] = both[0][:9]
    share[9:18] = both[1][:9]
    rest = both[0] + both[1]
    share[18:20] = rest[9:11] + (rest[11:13] + rest[13:15])

    def share_copy(o):
        return pltpu.make_async_remote_copy(
            share, shares.at[spot], ag_send.at[o - 1], ag_recv.at[o - 1],
            device_id=spot_id(o), device_id_type=MESH,
        )

    for o in sorted(range(1, 2 * ny), key=lambda o: -min(o, 2 * ny - o)):
        share_copy(o).start()
    own = pltpu.make_async_copy(share, shares.at[spot], put_sem.at[1])
    own.start()
    sent(0, dec_in)
    sent(1, send_c)
    sent(2, send_i)
    sent(3, send_d)
    sent(4, mail)
    for which, pad in enumerate((pad_c, pad_i, pad_a)):
        halo(which, pad, "sent")
    for to in range(nx):
        pl.when(to < x)(carry_copy(carry_a, carries_a, 0, to).wait_send)
        pl.when(to > x)(carry_copy(carry_s, carries_s, 1, to).wait_send)
    for h in range(2):
        core_copy(h).wait_send()

    @pl.loop(0, others)
    def _(i):
        xy_copy(i).wait_send()

    for o in range(1, 2 * ny):
        share_copy(o).wait_recv()
    own.wait()
    put_dinp.wait()

    for o in range(1, 2 * ny):
        share_copy(o).wait_send()


def finish(ny, ln, wscale, dscale, dinp_hbm, shares_hbm, out_hbm, din_ref, dout_ref, dg_ref, shares, tile, sem):
    fetch = pltpu.make_async_copy(shares_hbm, shares, sem.at[0])
    fetch.start()
    size = tile.shape[0] // 4
    parts = [pl.ds(i * size, size) for i in range(4)]
    comes = [
        pltpu.make_async_copy(dinp_hbm.at[part], tile.at[part], sem.at[1 + i])
        for i, part in enumerate(parts)
    ]
    goes = [
        pltpu.make_async_copy(tile.at[part], out_hbm.at[part], sem.at[5 + i])
        for i, part in enumerate(parts)
    ]
    for come in comes:
        come.start()
    for come, go in zip(comes, goes):
        come.wait()
        go.start()
    fetch.wait()
    for j in range(ny):
        both = shares[2 * j] + shares[2 * j + 1]
        din_ref[:, j] = both[:9] * wscale
        dout_ref[:, j] = both[9:18] * wscale
    total = shares[0, 18:20]
    for s in range(1, 2 * ny):
        total += shares[s, 18:20]
    dg_ref[:, :ln] = total[:1] * dscale
    dg_ref[:, ln:] = total[1:] * dscale
    for go in goes:
        go.wait()


def body(nx, inputs, cotangent, w_in, w_out, decay, skip):
    _, rows, wide, ln = inputs.shape
    ny = lax.axis_size("row")
    nz = lax.axis_size("tm") // nx
    states = w_in.shape[3]
    cells = 2 * rows
    block = cells * nz
    wscale = 1.0 / math.sqrt(nx * nz * ny * rows * wide * 2)
    dscale = 1.0 / math.sqrt(ny * rows * wide * 2)
    vmem = pltpu.VMEM
    dma = pltpu.SemaphoreType.DMA
    scratch = [
        vmem((rows, wide, ln), BF16),
        vmem((rows, wide, ln), BF16),
        vmem((9, ln, states), BF16),
        vmem((9, states, ln), BF16),
        vmem((1, states), F32),
        vmem((1, ln), F32),
        dma((6,)),
        vmem((block, ln), F32),
        vmem((nz, cells, ln), BF16),
        vmem((nz, cells, ln), BF16),
        vmem((nz, cells, ln), BF16),
        vmem((nz, cells, ln), BF16),
        vmem((nz, cells, ln), BF16),
        vmem((nz, cells, ln), BF16),
        vmem((nz, 1, states), F32),
        vmem((2, nz, ln), F32),
        vmem((4, rows + 2, nz, ln), BF16),
        vmem((4, rows + 2, nz, ln), BF16),
        vmem((4, rows + 2, nz, states), BF16),
        vmem((block, 9 * ln), BF16),
        vmem((block, 9 * ln), BF16),
        vmem((9 * ln, states), BF16),
        vmem((9 * ln, states), BF16),
        vmem((9, states, ln), BF16),
        vmem((2, block, ln), F32),
        vmem((2, block, ln), F32),
        vmem((2, cells + 16, ln), BF16),
        vmem((nx, 2, cells + 16, ln), BF16),
        vmem((2, cells + 16, ln), BF16),
        vmem((nx, 2, cells + 16, ln), BF16),
        vmem((2, cells, ln), F32),
        vmem((2, nz, ln), F32),
        vmem((2, ny, nx, nz, 9 * ln), F32),
        vmem((ny, nx, nz, 9 * ln), BF16),
        vmem((ny, nx, nz, 9 * ln), BF16),
        vmem((ny, nx, nz, 9 * ln), BF16),
        vmem((nx * ny - 1, nz, 9 * ln), BF16),
        vmem((nz, 16, ln), F32),
        vmem((nz, 16, ln), BF16),
        vmem((nz, 16, ln), BF16),
        vmem((20, ln), F32),
        vmem((rows, wide, ln), BF16),
        dma((2,)),
        dma((5,)),
        dma((5,)),
        dma((3, 8)),
        dma((3, 8)),
        dma((2, nx)),
        dma((2, nx)),
        dma((2,)),
        dma((2,)),
        dma((nx * ny - 1,)),
        dma((nx * ny - 1,)),
        dma((2 * ny - 1,)),
        dma((2 * ny - 1,)),
    ]
    tile = jax.ShapeDtypeStruct((rows, wide, ln), BF16)
    d_inputs, shares = pl.pallas_call(
        functools.partial(kernel, nx, nz, ny, rows, ln),
        out_shape=(tile, jax.ShapeDtypeStruct((2 * ny, 20, ln), F32)),
        in_specs=[pl.BlockSpec(memory_space=pltpu.HBM)] * 6,
        out_specs=(pl.BlockSpec(memory_space=pltpu.HBM), pl.BlockSpec(memory_space=pltpu.HBM)),
        scratch_shapes=scratch,
        compiler_params=pltpu.CompilerParams(
            collective_id=0, has_side_effects=True, vmem_limit_bytes=63 * 1024 * 1024
        ),
        cost_estimate=pl.CostEstimate(
            flops=5 * 2 * block * 9 * ln * states, bytes_accessed=4 * 1024 * 1024, transcendentals=0
        ),
    )(
        inputs.reshape(rows, wide, ln),
        cotangent.reshape(rows, wide, ln),
        w_in.reshape(9, ln, states),
        w_out.reshape(9, states, ln),
        decay,
        skip.reshape(1, ln),
    )
    whole = pl.BlockSpec(memory_space=pltpu.VMEM)
    d_inputs, d_in, d_out, d_decay = pl.pallas_call(
        functools.partial(finish, ny, ln, wscale, dscale),
        out_shape=(
            tile,
            jax.ShapeDtypeStruct((9, ny, ln), F32),
            jax.ShapeDtypeStruct((9, ny, ln), F32),
            jax.ShapeDtypeStruct((1, states), F32),
        ),
        in_specs=[pl.BlockSpec(memory_space=pltpu.HBM)] * 2,
        out_specs=(pl.BlockSpec(memory_space=pltpu.HBM), whole, whole, whole),
        scratch_shapes=[vmem((2 * ny, 20, ln), F32), vmem((rows, wide, ln), BF16), dma((9,))],
        compiler_params=pltpu.CompilerParams(vmem_limit_bytes=63 * 1024 * 1024),
    )(d_inputs, shares)

    def by_channel(grad):
        return jnp.transpose(grad.reshape(3, 3, ny, ln), (2, 0, 1, 3))

    return (d_inputs[None], by_channel(d_in), by_channel(d_out), d_decay)


def solution(mesh, nx=X_CHIPS):
    in_specs = (
        P("tm", "row", "col", None),
        P("tm", "row", "col", None),
        P(),
        P(),
        P("tm", None),
        P(),
    )
    out_specs = (
        P("tm", "row", "col", None),
        P("tm", None, None, None),
        P("tm", None, None, None),
        P("tm", None),
    )
    return jax.shard_map(
        functools.partial(body, nx), mesh=mesh, in_specs=in_specs, out_specs=out_specs,
        check_vma=False,
    )
```
